128 devices in a mesh: section: 2 (over z_hi), dp: 16 (over y, z_lo, core), tensor: 4 (over x).
Axes of the slice: x: 4, y: 4, z: 4 (z_hi: 2, z_lo: 2; z = z_hi * 2 + z_lo), core: 2. Of those that a mesh axis runs over, the one named last changes fastest.
Arguments:
- features: bfloat16 [4, 8192, 1280], P('section', ('dp', 'tensor')), may hold values from -6 to 6
- layer_norm_gain: float32 [4, 1280], P('section'), may hold values from 0.1 to 1.9
- layer_norm_bias: float32 [4, 1280], P('section'), may hold values from -3 to 3
- proj_weight: bfloat16 [5120, 8192], P('section', 'tensor'), may hold values from -0.078125 to 0.078125
- cotangent: bfloat16 [16, 512, 8192], P('dp', 'section', 'tensor'), may hold values from -6 to 6
Outputs:
- projected: bfloat16 [16, 512, 8192], P('dp', 'section', 'tensor')
- weight_grad: bfloat16 [5120, 8192], P('section', 'tensor')
- hidden_state_gradient: bfloat16 [4, 8192, 1280], P('section', ('dp', 'tensor'))
The draws below stay inside these ranges and needn't reach their ends.
All inputs are finite; a program needn't handle non-finite values.
Results may differ from the reference program's by a relative error of at most 0.022.
Values may be sent and summed in bfloat16 or wider, within the bound.
No kernel may reach another device: no remote copies, remote signals or barrier semaphores. Data moves between devices by JAX's collectives and lax.ppermute only.
A program may use at most 128 MiB of HBM per device.

```python
import jax
import jax.numpy as jnp
from jax import lax

VD = 1280
OUT = 8192
TAPS = 4
TOK_GROUP = 512
TOKENS = 8192
N_DP = 16


def shard_levels(key, dims, shards, smallest, largest):
    gain, own = 1.0, jax.random.fold_in(key, 6)
    for dim, parts in shards:
        draws = jnp.exp(jax.random.uniform(jax.random.fold_in(own, dim), (parts,), jnp.float32, smallest / len(shards), largest / len(shards)))
        gain = gain * jnp.repeat(draws, dims[dim] // parts).reshape([-1 if axis == dim else 1 for axis in range(len(dims))])
    return gain


def bell_draw(key, extent, scale, limit, shards=(), held_as=jnp.bfloat16):
    result = jax.random.normal(key, extent, jnp.float32) * scale
    if len(shards) > 0:
        result = shard_levels(key, extent, shards, -0.22, 0.18) * result
    return jnp.clip(result, min=-limit, max=limit).astype(held_as)


def setup_inputs(seed: int = 0) -> dict:
    splits = jax.random.split(jax.random.key(seed), 6)
    features = bell_draw(splits[0], (TAPS, TOKENS, VD), 1.0, 6.0, ((0, 2), (1, 64)))
    layer_norm_gain = jnp.clip(1.0 + 0.18 * jax.random.normal(splits[1], (TAPS, VD), jnp.float32), 0.1, 1.9)
    layer_norm_bias = bell_draw(splits[2], (TAPS, VD), 0.5, 3.0, ((0, 2),), jnp.float32)
    proj_weight = bell_draw(splits[3], (TAPS * VD, OUT), (TAPS * VD) ** -0.5, 0.078125, ((0, 2), (1, 4)))
    cotangent = bell_draw(splits[4], (N_DP, TOK_GROUP, OUT), 1.0, 6.0, ((0, 16), (1, 2), (2, 4)))
    return dict(features=features, layer_norm_gain=layer_norm_gain, layer_norm_bias=layer_norm_bias, proj_weight=proj_weight, cotangent=cotangent)


def apply_layer_norm(features, layer_norm_gain, layer_norm_bias):
    x = features.astype(jnp.float32)
    mu = lax.optimization_barrier(jnp.mean(x, axis=-1, keepdims=True))
    centered_rows = x - mu
    inverse_deviation = 1.0 / jnp.sqrt(lax.optimization_barrier(jnp.mean(centered_rows * centered_rows, axis=-1, keepdims=True)) + 1e-05)
    standardized_input = centered_rows * inverse_deviation
    norm_output = (standardized_input * layer_norm_gain[:, None, :] + layer_norm_bias[:, None, :]).astype(jnp.bfloat16)
    return (standardized_input, inverse_deviation, norm_output)

def reference(features, layer_norm_gain, layer_norm_bias, proj_weight, cotangent):
    standardized_input, inverse_deviation, norm_output = apply_layer_norm(features, layer_norm_gain, layer_norm_bias)
    weight = proj_weight.astype(jnp.float32).reshape(TAPS, VD, OUT)
    groups = norm_output.reshape(TAPS, N_DP, TOK_GROUP, VD)
    grads = cotangent.astype(jnp.float32)

    def per_group(total, index):
        rows = lax.dynamic_index_in_dim(groups, index, 1, keepdims=False).astype(jnp.float32)
        gcot = lax.dynamic_index_in_dim(grads, index, 0, keepdims=False)
        proj = jnp.einsum('lrc,lco->ro', rows, weight).astype(jnp.bfloat16)
        part = jnp.einsum('lrc,ro->lco', rows, gcot).astype(jnp.bfloat16)
        dn = jnp.einsum('ro,lco->lrc', gcot, weight)
        return (total + part.astype(jnp.float32), (proj, dn))
    total0 = jnp.zeros((TAPS, VD, OUT), jnp.float32)
    total, (projected, dnorm) = lax.scan(per_group, total0, jnp.arange(N_DP, dtype=jnp.int32))
    weight_grad = total.reshape(TAPS * VD, OUT).astype(jnp.bfloat16)
    dnorm = jnp.transpose(dnorm, (1, 0, 2, 3)).reshape(TAPS, TOKENS, VD)
    gain_scaled = dnorm * layer_norm_gain[:, None, :]
    hidden_state_gradient = inverse_deviation * (gain_scaled - lax.optimization_barrier(jnp.mean(gain_scaled, axis=-1, keepdims=True)) - standardized_input * lax.optimization_barrier(jnp.mean(gain_scaled * standardized_input, axis=-1, keepdims=True)))
    return (projected, weight_grad, hidden_state_gradient.astype(jnp.bfloat16))
```

```python
import jax
import jax.numpy as jnp
from jax import lax
from jax.experimental import pallas as pl
from jax.experimental.pallas import tpu as pltpu
from jax.sharding import PartitionSpec as P

F32 = jnp.float32
BF16 = jnp.bfloat16
VMEM_LIMIT = 48 * 1024 * 1024

ROW_CHUNKS = ((0, 512), (512, 768))


def dp_pairs(fy=lambda y: y, fz=lambda z: z, fc=lambda c: c):
    return [(i, fy(i // 4) * 4 + fz(i // 2 % 2) * 2 + fc(i % 2)) for i in range(16)]


Y1 = dp_pairs(fy=lambda y: y ^ 1)
Y3 = dp_pairs(fy=lambda y: y ^ 3)
ZLO = dp_pairs(fz=lambda z: z ^ 1)
CORE = dp_pairs(fc=lambda c: c ^ 1)
SECTION = [(0, 1), (1, 0)]
AROUND, SLOTS = 1, 5


def shift(step):
    return [(i, (i + step) % 4) for i in range(4)]


def swap(value, pairs, axis="dp"):
    return lax.ppermute(value, axis, pairs)


def index_vector():
    s, d, x = lax.axis_index("section"), lax.axis_index("dp"), lax.axis_index("tensor")
    y = d // 4
    slots = [(t // 2 ^ s) * 2 + t % 2 for t in (x, (x + 1) % 4, (x + 3) % 4, (x + 2) % 4)]
    return jnp.stack([d % 2, y, y ^ 1, y ^ 2, y ^ 3, *slots]).astype(jnp.int32)


def call(kernel, index, operands, in_specs, out_shapes, out_specs, grid, flops=0, scratch=(), aliases=None):
    read = sum(a.size * a.dtype.itemsize for a in operands)
    written = sum(a.size * a.dtype.itemsize for a in out_shapes)
    return pl.pallas_call(
        kernel,
        grid_spec=pltpu.PrefetchScalarGridSpec(
            num_scalar_prefetch=1,
            grid=grid,
            in_specs=in_specs,
            out_specs=out_specs,
            scratch_shapes=scratch,
        ),
        out_shape=out_shapes,
        input_output_aliases=aliases or {},
        compiler_params=pltpu.CompilerParams(vmem_limit_bytes=VMEM_LIMIT),
        cost_estimate=pl.CostEstimate(flops=flops, bytes_accessed=read + written, transcendentals=0),
    )(index, *operands)


def full(array):
    return pl.BlockSpec(array.shape, lambda *_: (0,) * len(array.shape))


def out(*shape, dtype=BF16):
    return jax.ShapeDtypeStruct(shape, dtype)


def dot(a, b, contract=(1, 0)):
    return lax.dot_general(a, b, (((contract[0],), (contract[1],)), ((), ())), preferred_element_type=F32)


def moments(value):
    mean = jnp.mean(value, axis=-1, keepdims=True)
    centered = value - mean
    inverse = 1.0 / jnp.sqrt(jnp.mean(centered * centered, axis=-1, keepdims=True) + 1e-05)
    return centered * inverse, inverse


def normalize(index, features, theirs, gain, bias):
    _, rows, width = features.shape

    def kernel(index_ref, own_ref, theirs_ref, gain_ref, bias_ref, *outs):
        c = index_ref[0]
        gain, bias = gain_ref[pl.ds(c, 1)], bias_ref[pl.ds(c, 1)]
        for k, value in enumerate((own_ref[0], theirs_ref[...])):
            standard, _ = moments(value.astype(F32))
            normed = (standard * gain + bias).astype(BF16)
            for (start, size), out_ref in zip(ROW_CHUNKS, outs):
                out_ref[k] = normed[:, start : start + size]

    shapes = [out(2, rows, size) for _, size in ROW_CHUNKS]
    return call(
        kernel,
        index,
        [features, theirs, gain, bias],
        [pl.BlockSpec((1, rows, width), lambda i, idx: (idx[0], 0, 0)), full(theirs), full(gain), full(bias)],
        shapes,
        [full(s) for s in shapes],
        (1,),
    )


def normalize_backward(index, features, theirs, gain, parts):
    _, rows, width = features.shape

    def kernel(index_ref, own_ref, theirs_ref, gain_ref, *refs):
        gain = gain_ref[pl.ds(index_ref[0], 1)]
        for k, value in enumerate((own_ref[0], theirs_ref[...])):
            standard, inverse = moments(value.astype(F32))
            total = refs[0][k].astype(F32)
            for ref in refs[1:-1]:
                total = total + ref[k].astype(F32)
            scaled = total * gain
            hidden = inverse * (
                scaled
                - jnp.mean(scaled, axis=-1, keepdims=True)
                - standard * jnp.mean(scaled * standard, axis=-1, keepdims=True)
            )
            refs[-1][k] = hidden.astype(BF16)

    shape = out(2, rows, width)
    return call(
        kernel,
        index,
        [features, theirs, gain, *parts],
        [pl.BlockSpec((1, rows, width), lambda i, idx: (idx[0], 0, 0)), full(theirs), full(gain)]
        + [full(p) for p in parts],
        [shape],
        [full(shape)],
        (1,),
    )[0]


def transpose_pieces(index_ref, pieces, scratch):
    for n, piece in enumerate(pieces):
        for k in range(2):
            at = pl.multiple_of((4 * k + index_ref[SLOTS + n]) * 128, 128)
            scratch[:, pl.ds(at, 128)] = piece[k].T


def weight_grad_blocks(index, pieces, grads, blocks, wanted):
    rows = pieces[0].shape[2]
    half = rows // 2
    part = grads[0].shape[1] // 4
    steps = len(blocks)

    def kernel(index_ref, *refs):
        ins, gs = refs[:4], refs[4:8]
        outs, scratch = refs[8:-1], refs[-1]
        step = pl.program_id(0)

        @pl.when(step == 0)
        def _():
            transpose_pieces(index_ref, ins, scratch)

        for k, block in enumerate(blocks):
            @pl.when(step == k)
            def _(block=block):
                for which, out_ref in zip(wanted, outs):
                    h, held, dtype = which
                    if block not in held:
                        continue
                    mine = scratch[h * half : (h + 1) * half]
                    total = dot(mine[:, :256], gs[0][...])
                    for p in range(1, 4):
                        total = total + dot(mine[:, 256 * p : 256 * (p + 1)], gs[p][...])
                    out_ref[...] = total.astype(dtype)

    def pick(values):
        def index_map(i, idx):
            result = jnp.int32(values[0])
            for k in range(1, steps):
                result = jnp.where(i >= k, jnp.int32(values[k]), result)
            return (0, result)

        return index_map

    out_specs = []
    for h, held, _ in wanted:
        place, last = [], 0
        for block in blocks:
            if block in held:
                last = held.index(block)
            place.append(last)
        out_specs.append(pl.BlockSpec((half, part), pick(place)))
    shapes = [out(half, len(held) * part, dtype=dtype) for _, held, dtype in wanted]
    return call(
        kernel,
        index,
        [*pieces, *grads],
        [full(p) for p in pieces] + [pl.BlockSpec((256, part), pick(blocks))] * 4,
        shapes,
        out_specs,
        (steps,),
        flops=2 * 1024 * half * part * sum(len(held) for _, held, _ in wanted),
        scratch=[pltpu.VMEM((rows, 1024), BF16)],
    )


def row_gradients(index, grads, proj_weight):
    part = grads[0].shape[1] // 4
    width = proj_weight.shape[0] // 2

    def kernel(index_ref, *refs):
        gs, w, outs, acc = refs[:4], refs[4], refs[5:9], refs[9]
        step = pl.program_id(0)
        for p in range(4):
            rows = slice(256 * p, 256 * (p + 1))
            value = dot(gs[p][...], w[...], (1, 1))

            @pl.when(step == 0)
            def _():
                acc[rows] = value

            @pl.when(step > 0)
            def _():
                acc[rows] = acc[rows] + value

        @pl.when(step == 3)
        def _():
            for n, out_ref in enumerate(outs):
                for k in range(2):
                    at = pl.multiple_of((4 * k + index_ref[SLOTS + n]) * 128, 128)
                    out_ref[k] = acc[pl.ds(at, 128)].astype(BF16)

    shapes = [out(2, 128, width)] * 4
    return call(
        kernel,
        index,
        [*grads, proj_weight],
        [pl.BlockSpec((256, part), lambda i, idx: (0, i))] * 4
        + [pl.BlockSpec((width, part), lambda i, idx: (idx[0], idx[AROUND + i]))],
        shapes,
        [full(s) for s in shapes],
        (4,),
        flops=2 * 1024 * width * part * 4,
        scratch=[pltpu.VMEM((1024, width), F32)],
    )


def project(index, chunks, proj_weight):
    width, cols = proj_weight.shape[0] // 2, proj_weight.shape[1]
    part = cols // 4
    count = len(chunks)

    def kernel(index_ref, *refs):
        ins, w, own, other, scratch = refs[: 4 * count], refs[-4], refs[-3], refs[-2], refs[-1]

        @pl.when(pl.program_id(0) == 0)
        def _():
            for m, (start, size) in enumerate(ROW_CHUNKS):
                for n in range(4):
                    for k in range(2):
                        at = pl.multiple_of((4 * k + index_ref[SLOTS + n]) * 128, 128)
                        scratch[pl.ds(at, 128), start : start + size] = ins[4 * m + n][k]

        own[...] = dot(scratch[:512], w[...]).astype(BF16)
        other[...] = dot(scratch[512:], w[...]).astype(BF16)

    operands = [piece for chunk in chunks for piece in chunk]
    shapes = [out(512, cols)] * 2
    return call(
        kernel,
        index,
        [*operands, proj_weight],
        [full(p) for p in operands] + [pl.BlockSpec((width, part), lambda i, idx: (idx[0], i))],
        shapes,
        [pl.BlockSpec((512, part), lambda i, idx: (0, i))] * 2,
        (4,),
        flops=2 * 1024 * width * cols,
        scratch=[pltpu.VMEM((1024, width), BF16)],
    )


def place(index, pieces, start, size, width, cols, into):
    half, part = size // 2, cols // 4
    count = len(pieces)

    def kernel(index_ref, *refs):
        sources, result, sems = refs[:count], refs[-2], refs[-1]
        c = index_ref[0]
        at = [pl.ds(pl.multiple_of(index_ref[AROUND + j] * part, part), part) for j in range(4)]
        left, right, every = slice(0, part), slice(part, 2 * part), slice(None)
        copies = []
        for k, tap in enumerate((c, 1 - c)):
            a = pl.ds(pl.multiple_of(tap * width + start, 128), half)
            b = pl.ds(pl.multiple_of(tap * width + start + half, 128), half)
            for n, src, dst in (
                (0, (slice(0, half), every), (a, at[0])),
                (0, (slice(half, size), every), (b, at[0])),
                (1, (every, every), (a, at[3])),
                (2, (every, every), (b, at[1])),
                (3, (every, left), (a, at[1])),
                (3, (every, right), (a, at[2])),
                (4, (every, left), (b, at[3])),
                (4, (every, right), (b, at[2])),
            ):
                copies.append(
                    pltpu.make_async_copy(sources[5 * k + n].at[src], result.at[dst], sems.at[len(copies)])
                )
        for copy in copies:
            copy.start()
        for copy in copies:
            copy.wait()

    anywhere = pl.BlockSpec(memory_space=pl.ANY)
    operands = list(pieces) + ([] if into is None else [into])
    return call(
        kernel,
        index,
        operands,
        [full(p) for p in pieces] + ([] if into is None else [anywhere]),
        [out(2 * width, cols)],
        [anywhere],
        (1,),
        scratch=[pltpu.SemaphoreType.DMA((16,))],
        aliases={} if into is None else {count + 1: 0},
    )[0]


def body(features, layer_norm_gain, layer_norm_bias, proj_weight, cotangent):
    index = index_vector()
    c = index[0]
    width = layer_norm_gain.shape[1]
    cols = proj_weight.shape[1]
    part = cols // 4

    mine = jnp.concatenate(
        [lax.dynamic_slice(cotangent[0], (0, index[AROUND + j] * part), (256, part)) for j in range(4)], axis=1
    )
    away = swap(mine, SECTION, "section")
    grads = [mine, away, swap(mine, CORE), swap(away, CORE)]

    theirs = swap(lax.dynamic_index_in_dim(features, 1 - c, 0, keepdims=False), CORE)
    gathered = [
        [mine] + [swap(mine, shift(k), "tensor") for k in (-1, 1, 2)]
        for mine in normalize(index, features, theirs, layer_norm_gain, layer_norm_bias)
    ]

    weight_grad = None
    for (r0, size), pieces in zip(ROW_CHUNKS, gathered):
        half = size // 2
        send_a, send_b = weight_grad_blocks(
            index, pieces, grads, (1, 2, 3), ((0, (1, 2), BF16), (1, (2, 3), BF16))
        )
        got_a, got_b = swap(send_a, Y1), swap(send_b, Y3)
        next_a, next_b, keep_a, keep_b = weight_grad_blocks(
            index, pieces, grads, (3, 1, 0), ((0, (3,), F32), (1, (1,), F32), (0, (0,), F32), (1, (0,), F32))
        )
        next_a = (next_a + got_a[:, part:].astype(F32)).astype(BF16)
        next_b = (next_b + got_b[:, :part].astype(F32)).astype(BF16)
        more_a, more_b = swap(next_a, Y3), swap(next_b, Y1)
        keep_a = keep_a + got_a[:, :part].astype(F32) + more_a.astype(F32)
        keep_b = keep_b + got_b[:, part:].astype(F32) + more_b.astype(F32)
        keep = lax.optimization_barrier(jnp.concatenate([keep_a, keep_b], axis=0).astype(BF16))
        done = (keep.astype(F32) + swap(keep, ZLO).astype(F32)).astype(BF16)
        done_a, done_b = done[:half], done[half:]
        second_a, second_b = swap(done_a, Y3), swap(done_b, Y1)
        last_a = swap(jnp.concatenate([done_a, second_a], axis=1), Y1)
        last_b = swap(jnp.concatenate([done_b, second_b], axis=1), Y3)
        ours = [done, second_a, second_b, last_a, last_b]
        weight_grad = place(
            index, ours + [swap(m, CORE) for m in ours], r0, size, width, cols, weight_grad
        )

    parts = row_gradients(index, grads, proj_weight)
    parts = [parts[0]] + [swap(p, shift(k), "tensor") for p, k in zip(parts[1:], (1, -1, 2))]
    hidden = normalize_backward(index, features, theirs, layer_norm_gain, parts)
    ours, back = hidden[0], swap(hidden[1], CORE)
    hidden = jnp.where(c == 0, jnp.stack([ours, back]), jnp.stack([back, ours]))

    own, other = project(index, gathered, proj_weight)
    other = swap(other, CORE)
    back = swap((own[256:].astype(F32) + other[256:].astype(F32)).astype(BF16), SECTION, "section")
    projected = own[:256].astype(F32) + other[:256].astype(F32) + back.astype(F32)
    return (projected.astype(BF16)[None], weight_grad, hidden)


def solution(mesh):
    return jax.shard_map(
        body,
        mesh=mesh,
        in_specs=(
            P("section", ("dp", "tensor"), None),
            P("section", None),
            P("section", None),
            P("section", "tensor"),
            P("dp", "section", "tensor"),
        ),
        out_specs=(
            P("dp", "section", "tensor"),
            P("section", "tensor"),
            P("section", ("dp", "tensor"), None),
        ),
        check_vma=False,
    )
```

```python
import jax
import jax.numpy as jnp
from jax import lax
from jax.experimental import pallas as pl
from jax.experimental.pallas import tpu as pltpu
from jax.sharding import PartitionSpec as P

F32 = jnp.float32
BF16 = jnp.bfloat16
VMEM_LIMIT = 20 * 1024 * 1024

ROW_CHUNKS = ((0, 640), (640, 640))


def dp_pairs(fy=lambda y: y, fz=lambda z: z, fc=lambda c: c):
    return [(i, fy(i // 4) * 4 + fz(i // 2 % 2) * 2 + fc(i % 2)) for i in range(16)]


Y1 = dp_pairs(fy=lambda y: y ^ 1)
Y3 = dp_pairs(fy=lambda y: y ^ 3)
ZLO = dp_pairs(fz=lambda z: z ^ 1)
CORE = dp_pairs(fc=lambda c: c ^ 1)
SECTION = [(0, 1), (1, 0)]
AROUND, SLOT_OF, SLOTS = 1, 5, 9


def shift(step):
    return [(i, (i + step) % 4) for i in range(4)]


def swap(value, pairs, axis="dp"):
    return lax.ppermute(value, axis, pairs)


ANY = pl.BlockSpec(memory_space=pl.ANY)
HBM = pl.BlockSpec(memory_space=pltpu.HBM)


class Copies:
    def __init__(self, sems):
        self.sems, self.all = sems, []

    def start(self, *pairs):
        copies = []
        for source, target in pairs:
            copies.append(pltpu.make_async_copy(source, target, self.sems.at[len(self.all)]))
            copies[-1].start()
            self.all.append(copies[-1])
        return copies


def wait(*groups):
    for group in groups:
        for copy in group:
            copy.wait()


def prepare(features, cotangent):
    _, rows, width = features.shape
    _, tokens, cols = cotangent.shape
    part = cols // 4

    def kernel(features_hbm, cotangent_hbm, theirs_out, mine_out, index_out, theirs, mine, sems):
        s, d = lax.axis_index("section"), lax.axis_index("dp")
        y, c = d // 4, d % 2
        around = (y, y + 1 - 2 * (y % 2), (y + 2) % 4, 3 - y)
        copies = Copies(sems)
        first = copies.start((features_hbm.at[1 - c], theirs))
        blocks = []
        for n, j in enumerate(around):
            at = pl.ds(pl.multiple_of(j * part, part), part)
            blocks.append(copies.start((cotangent_hbm.at[0, :, at], mine.at[:, n * part : (n + 1) * part])))
        index_out[0] = c
        for n, j in enumerate(around):
            index_out[AROUND + n] = j
        for t in range(4):
            index_out[SLOT_OF + t] = (s if t < 2 else 1 - s) * 2 + t % 2
        x = lax.axis_index("tensor")
        for n, t in enumerate((x, (x + 1) % 4, (x + 3) % 4, (x + 2) % 4)):
            index_out[SLOTS + n] = ((t // 2 + s) % 2) * 2 + t % 2
        wait(first)
        second = copies.start((theirs, theirs_out))
        for n, block in enumerate(blocks):
            wait(block)
            here = (slice(None), slice(n * part, (n + 1) * part))
            second += copies.start((mine.at[here], mine_out.at[here]))
        wait(second)

    return pl.pallas_call(
        kernel,
        in_specs=[HBM, HBM],
        out_specs=[ANY, ANY, pl.BlockSpec(memory_space=pltpu.SMEM)],
        out_shape=[out(rows, width), out(tokens, cols), out(13, dtype=jnp.int32)],
        scratch_shapes=[
            pltpu.VMEM((rows, width), BF16),
            pltpu.VMEM((tokens, cols), BF16),
            pltpu.SemaphoreType.DMA((10,)),
        ],
        compiler_params=pltpu.CompilerParams(vmem_limit_bytes=VMEM_LIMIT),
        cost_estimate=pl.CostEstimate(flops=1, bytes_accessed=1, transcendentals=0),
    )(features, cotangent)


def sums(*wanted, stack=False):
    flat = [(a, at) for terms in wanted for a, at in terms]
    shapes = [out(*jax.eval_shape(lambda a, at=terms[0][1]: a[at], terms[0][0]).shape) for terms in wanted]
    count = len(flat)
    made = [out(len(shapes) * shapes[0].shape[0], *shapes[0].shape[1:])] if stack else shapes

    def kernel(*refs):
        ins, outs = refs[:count], refs[count : count + len(made)]
        held, results, sems = refs[count + len(made) : -1 - len(wanted)], refs[-1 - len(wanted) : -1], refs[-1]
        if stack:
            rows = shapes[0].shape[0]
            outs = [outs[0].at[n * rows : (n + 1) * rows] for n in range(len(shapes))]
        copies = Copies(sems)
        arrived = [copies.start((ref.at[at], to)) for ref, (_, at), to in zip(ins, flat, held)]
        done, n = [], 0
        for terms, result, out_ref in zip(wanted, results, outs):
            total = None
            for _ in terms:
                wait(arrived[n])
                value = held[n][...].astype(F32)
                total = value if total is None else total + value
                n += 1
            result[...] = total.astype(BF16)
            done += copies.start((result, out_ref))
        wait(done)

    held_shapes = [s for terms, s in zip(wanted, shapes) for _ in terms]
    return pl.pallas_call(
        kernel,
        in_specs=[ANY] * count,
        out_specs=[ANY] * len(made),
        out_shape=made,
        scratch_shapes=[
            *(pltpu.VMEM(s.shape, BF16) for s in held_shapes),
            *(pltpu.VMEM(s.shape, BF16) for s in shapes),
            pltpu.SemaphoreType.DMA((count + len(shapes),)),
        ],
        compiler_params=pltpu.CompilerParams(vmem_limit_bytes=VMEM_LIMIT),
        cost_estimate=pl.CostEstimate(flops=1, bytes_accessed=1, transcendentals=0),
    )(*(a for a, _ in flat))


def call(kernel, index, operands, in_specs, out_shapes, out_specs, grid, scratch=(), aliases=None):
    return pl.pallas_call(
        kernel,
        grid_spec=pltpu.PrefetchScalarGridSpec(
            num_scalar_prefetch=1,
            grid=grid,
            in_specs=in_specs,
            out_specs=out_specs,
            scratch_shapes=scratch,
        ),
        out_shape=out_shapes,
        input_output_aliases=aliases or {},
        compiler_params=pltpu.CompilerParams(vmem_limit_bytes=VMEM_LIMIT),
        cost_estimate=pl.CostEstimate(flops=1, bytes_accessed=1, transcendentals=0),
    )(index, *operands)


def full(array):
    return pl.BlockSpec(array.shape, lambda *_: (0,) * len(array.shape))


def out(*shape, dtype=BF16):
    return jax.ShapeDtypeStruct(shape, dtype)


def dot(a, b, contract=(1, 0)):
    return lax.dot_general(a, b, (((contract[0],), (contract[1],)), ((), ())), preferred_element_type=F32)


def moments(value):
    mean = jnp.mean(value, axis=-1, keepdims=True)
    centered = value - mean
    inverse = 1.0 / jnp.sqrt(jnp.mean(centered * centered, axis=-1, keepdims=True) + 1e-05)
    return centered * inverse, inverse


def normalize(index, features, theirs, gain, bias):
    _, rows, width = features.shape

    def kernel(index_ref, own_hbm, theirs_any, gain_hbm, bias_hbm, *refs):
        outs, (held, scale, normed, sems) = refs[:-4], refs[-4:]
        c = index_ref[0]
        copies = Copies(sems)
        first = copies.start((gain_hbm, scale.at[0]), (bias_hbm, scale.at[1]))
        arrived = [copies.start((own_hbm.at[c], held.at[0])), copies.start((theirs_any, held.at[1]))]
        wait(first)
        gain, bias = scale[0, pl.ds(c, 1)], scale[1, pl.ds(c, 1)]
        done = []
        for k in range(2):
            wait(arrived[k])
            standard, _ = moments(held[k].astype(F32))
            normed[k] = (standard * gain + bias).astype(BF16)
            for (start, size), out_ref in zip(ROW_CHUNKS, outs):
                done += copies.start((normed.at[k, :, start : start + size], out_ref.at[k]))
        wait(done)

    shapes = [out(2, rows, size) for _, size in ROW_CHUNKS]
    return call(
        kernel,
        index,
        [features, theirs, gain, bias],
        [HBM, ANY, HBM, HBM],
        shapes,
        [ANY] * len(shapes),
        (1,),
        scratch=[
            pltpu.VMEM((2, rows, width), BF16),
            pltpu.VMEM((2, *gain.shape), F32),
            pltpu.VMEM((2, rows, width), BF16),
            pltpu.SemaphoreType.DMA((8,)),
        ],
    )


def normalize_backward(index, features, theirs, gain, parts):
    _, rows, width = features.shape

    def kernel(index_ref, own_ref, theirs_ref, gain_ref, *refs):
        gain = gain_ref[pl.ds(index_ref[0], 1)]
        for k, value in enumerate((own_ref[0], theirs_ref[...])):
            standard, inverse = moments(value.astype(F32))
            total = refs[0][k].astype(F32)
            for ref in refs[1:-1]:
                total = total + ref[k].astype(F32)
            scaled = total * gain
            hidden = inverse * (
                scaled
                - jnp.mean(scaled, axis=-1, keepdims=True)
                - standard * jnp.mean(scaled * standard, axis=-1, keepdims=True)
            )
            refs[-1][k] = hidden.astype(BF16)

    shape = out(2, rows, width)
    return call(
        kernel,
        index,
        [features, theirs, gain, *parts],
        [pl.BlockSpec((1, rows, width), lambda i, idx: (idx[0], 0, 0)), full(theirs), full(gain)]
        + [full(p) for p in parts],
        [shape],
        [full(shape)],
        (1,),
    )[0]


def weight_grad_blocks(index, normed, grads, wanted):
    rows = normed[0].shape[-1]
    stacked = len(normed) == 1
    count = len(normed)
    half = rows // 2
    part = grads[0].shape[1] // 4
    shapes = [out(half, blocks * part, dtype=dtype) for _, _, blocks, dtype in wanted]

    def kernel(index_ref, *refs):
        normed_hbm, gs, outs = refs[:count], refs[count : count + 4], refs[count + 4 : count + 4 + len(wanted)]
        held, turned, grad, *results, sems = refs[count + 4 + len(wanted) :]
        copies = Copies(sems)
        rows_in = {}
        for t in range(4):
            for k in range(2):
                source = normed_hbm[0].at[t, k] if stacked else normed_hbm[t].at[k]
                rows_in[t, k] = copies.start((source, held.at[t, k]))
        grads_in = {}
        for j in (2, 1, 3, 0):
            for n in range(4):
                source = gs[n].at[:, j * part : (j + 1) * part]
                target = grad.at[256 * n : 256 * (n + 1), j * part : (j + 1) * part]
                grads_in.setdefault(j, []).extend(copies.start((source, target)))
        for t in range(4):
            for k in range(2):
                wait(rows_in[t, k])
                at = pl.multiple_of((4 * k + index_ref[(SLOT_OF if stacked else SLOTS) + t]) * 128, 128)
                turned[:, pl.ds(at, 128)] = held[t, k].T
        copies_out = []
        for (h, first, blocks, dtype), out_ref, result in zip(wanted, outs, results):
            for j in range(first, first + blocks):
                wait(grads_in.pop(j, []))
            mine = turned[h * half : (h + 1) * half]
            result[...] = dot(mine, grad[:, first * part : (first + blocks) * part]).astype(dtype)
            for k in range(blocks):
                where = (slice(None), slice(k * part, (k + 1) * part))
                copies_out += copies.start((result.at[where], out_ref.at[where]))
        wait(copies_out)

    return call(
        kernel,
        index,
        [*normed, *grads],
        [ANY] * (count + 4),
        shapes,
        [ANY] * len(shapes),
        (1,),
        scratch=[
            pltpu.VMEM((4, *normed[0].shape[-3:]), BF16),
            pltpu.VMEM((rows, 1024), BF16),
            pltpu.VMEM((1024, 4 * part), BF16),
            *(pltpu.VMEM(s.shape, s.dtype) for s in shapes),
            pltpu.SemaphoreType.DMA((24 + sum(blocks for _, _, blocks, _ in wanted),)),
        ],
    )


def row_gradients(index, grads, proj_weight):
    cols = proj_weight.shape[1]
    part = cols // 4
    width = proj_weight.shape[0] // 2
    tile = 256

    def kernel(index_ref, *refs):
        gs, w, result, held, acc, sems = refs[:4], refs[4], refs[5:9], refs[9], refs[10], refs[11]

        @pl.when(pl.program_id(0) == 0)
        def _():
            copies = Copies(sems)
            for j in range(4):
                at = pl.multiple_of(index_ref[AROUND + j] * part, part)
                for n in range(4):
                    source = gs[n].at[:, j * part : (j + 1) * part]
                    copies.start((source, held.at[256 * n : 256 * (n + 1), pl.ds(at, part)]))
            wait(copies.all)

        acc[...] = dot(held[...], w[...], (1, 1)).astype(BF16)
        for t in range(4):
            for k in range(2):
                at = pl.multiple_of((4 * k + index_ref[SLOTS + t]) * 128, 128)
                result[t][k] = acc[pl.ds(at, 128)]

    shapes = [out(2, 128, width)] * 4
    return call(
        kernel,
        index,
        [*grads, proj_weight],
        [ANY] * 4 + [pl.BlockSpec((tile, cols), lambda i, idx: (idx[0] * (width // tile) + i, 0))],
        shapes,
        [pl.BlockSpec((2, 128, tile), lambda i, idx: (0, 0, i))] * 4,
        (width // tile,),
        scratch=[pltpu.VMEM((1024, cols), BF16), pltpu.VMEM((1024, tile), BF16), pltpu.SemaphoreType.DMA((16,))],
    )


def project(index, chunks, proj_weight):
    width, cols = proj_weight.shape[0] // 2, proj_weight.shape[1]
    flat = [piece for chunk in chunks for piece in chunk]
    count = len(flat)
    part = cols // 4

    def kernel(index_ref, *refs):
        ins, w_hbm, own, other = refs[:count], refs[count], refs[count + 1], refs[count + 2]
        held, w, result, sems = refs[count + 3 :]
        copies = Copies(sems)
        base = index_ref[0] * width

        def weights(i):
            pairs = []
            for k in range(4):
                rows = pl.ds(pl.multiple_of(base + k * (width // 4), width // 4), width // 4)
                here = slice(i * part, (i + 1) * part)
                pairs.append((w_hbm.at[rows, here], w.at[k * (width // 4) : (k + 1) * (width // 4), here]))
            return copies.start(*pairs)

        weights_in = [weights(0)]
        rows_in = []
        for m, (first, size) in enumerate(ROW_CHUNKS):
            pieces = ins[sum(len(chunk) for chunk in chunks[:m]) :][: len(chunks[m])]
            for t in range(4):
                for k in range(2):
                    stacked = len(pieces) == 1
                    slot = index_ref[(SLOT_OF if stacked else SLOTS) + t]
                    at = pl.multiple_of((4 * k + slot) * 128, 128)
                    source = pieces[0].at[t, k] if stacked else pieces[t].at[k]
                    rows_in += copies.start((source, held.at[pl.ds(at, 128), first : first + size]))
        weights_in += [weights(i) for i in range(1, 4)]
        wait(rows_in)
        copies_out = []
        for i in range(4):
            wait(weights_in[i])
            here = slice(i * part, (i + 1) * part)
            for rows, target in ((slice(512, 1024), other), (slice(0, 512), own)):
                result[rows, here] = dot(held[rows], w[:, here]).astype(BF16)
                copies_out += copies.start((result.at[rows, here], target.at[:, here]))
        wait(copies_out)

    shapes = [out(512, cols)] * 2
    return call(
        kernel,
        index,
        [*flat, proj_weight],
        [ANY] * (count + 1),
        shapes,
        [ANY] * 2,
        (1,),
        scratch=[
            pltpu.VMEM((1024, width), BF16),
            pltpu.VMEM((width, cols), BF16),
            pltpu.VMEM((1024, cols), BF16),
            pltpu.SemaphoreType.DMA((24 + 8 * len(chunks),)),
        ],
    )


EVERY = slice(None)


def add_first(next_a, next_b, got_a, got_b):
    part = next_a.shape[1]
    left, right = (EVERY, slice(0, part)), (EVERY, slice(part, 2 * part))
    return sums([(next_a, (EVERY, EVERY)), (got_a, right)], [(next_b, (EVERY, EVERY)), (got_b, left)])


def add_second(keep_a, keep_b, got_a, got_b, more_a, more_b):
    part = keep_a.shape[1]
    whole, left, right = (EVERY, EVERY), (EVERY, slice(0, part)), (EVERY, slice(part, 2 * part))
    return sums(
        [(keep_a, whole), (got_a, left), (more_a, whole)],
        [(keep_b, whole), (got_b, right), (more_b, whole)],
        stack=True,
    )[0]


def add_third(keep, other):
    half = keep.shape[0] // 2
    top, bottom = (slice(0, half), EVERY), (slice(half, 2 * half), EVERY)
    return sums([(keep, top), (other, top)], [(keep, bottom), (other, bottom)])


def join(left_a, left_b, right_a, right_b):
    half, part = left_a.shape

    def kernel(*refs):
        ins, outs, held, sems = refs[:4], refs[4:7], refs[7], refs[8]
        copies = Copies(sems)
        arrived = [
            copies.start((ref, held.at[n % 2, :, (n // 2) * part : (n // 2 + 1) * part])) for n, ref in enumerate(ins)
        ]
        done = []
        for n in range(2):
            wait(arrived[n], arrived[n + 2])
            done += copies.start((held.at[n], outs[n]), (held.at[n], outs[2].at[n * half : (n + 1) * half]))
        wait(done)

    return pl.pallas_call(
        kernel,
        in_specs=[ANY] * 4,
        out_specs=[ANY] * 3,
        out_shape=[out(half, 2 * part), out(half, 2 * part), out(2 * half, 2 * part)],
        scratch_shapes=[pltpu.VMEM((2, half, 2 * part), BF16), pltpu.SemaphoreType.DMA((8,))],
        compiler_params=pltpu.CompilerParams(vmem_limit_bytes=VMEM_LIMIT),
        cost_estimate=pl.CostEstimate(flops=1, bytes_accessed=1, transcendentals=0),
    )(left_a, left_b, right_a, right_b)


def place(index, pieces, start, width, cols, into):
    part = cols // 4
    half = next(size for first, size in ROW_CHUNKS if first == start) // 2
    arrays = []
    for piece in pieces:
        if not any(piece[0] is a for a in arrays):
            arrays.append(piece[0])
    which = [next(k for k, a in enumerate(arrays) if a is piece[0]) for piece in pieces]
    count = len(arrays)

    def kernel(index_ref, *refs):
        sources, result = refs[:count], refs[-3]
        held, sems = refs[-2], refs[-1]
        copies = Copies(sems)
        blocks = (slice(0, part), slice(part, 2 * part))
        arrived = [
            [copies.start((sources[k].at[row : row + half, b], held.at[n, :, b])) for b in blocks]
            for n, (k, (_, row, _, _, _)) in enumerate(zip(which, pieces))
        ]
        placed = []
        for n, (_, _, other, h, js) in enumerate(pieces):
            tap = 1 - index_ref[0] if other else index_ref[0]
            rows = pl.ds(pl.multiple_of(tap * width + start + h * half, 64), half)
            for b, j, ready in zip(blocks, js, arrived[n]):
                wait(ready)
                at = pl.ds(pl.multiple_of(index_ref[AROUND + j] * part, part), part)
                placed += copies.start((held.at[n, :, b], result.at[rows, at]))
        wait(placed)

    operands = arrays + ([] if into is None else [into])
    return call(
        kernel,
        index,
        operands,
        [ANY] * len(operands),
        [out(2 * width, cols)],
        [ANY],
        (1,),
        scratch=[pltpu.VMEM((len(pieces), half, 2 * part), BF16), pltpu.SemaphoreType.DMA((4 * len(pieces),))],
        aliases={} if into is None else {count + 1: 0},
    )[0]


class Phases:
    def __init__(self):
        self.here, self.away = {}, {}

    def __getitem__(self, name):
        return self.here[name]

    def __setitem__(self, name, value):
        self.here[name] = value

    def send(self, name, source, pairs, axis="dp"):
        self.away[name] = swap(self.here[source], pairs, axis)

    def land(self, *names):
        for name in names:
            self.here[name] = self.away.pop(name)

    def end(self, *drop):
        for name in drop:
            del self.here[name]
        self.here = lax.optimization_barrier(self.here)


def body(features, layer_norm_gain, layer_norm_bias, proj_weight, cotangent):
    width = layer_norm_gain.shape[1]
    cols = proj_weight.shape[1]
    half = ROW_CHUNKS[0][1] // 2
    wanted = (
        (0, 1, 2, BF16),
        (1, 2, 2, BF16),
        (0, 3, 1, BF16),
        (1, 1, 1, BF16),
        (0, 0, 1, BF16),
        (1, 0, 1, BF16),
    )
    v = Phases()

    def near(n):
        return [v["n%d" % n], *(v["x%d%d" % (n, k)] for k in (1, 3, 2))]

    def grads():
        return [v["mine"], v["away"], v["mine_c"], v["away_c"]]

    def products(t):
        names = "send_a", "send_b", "next_a", "next_b", "keep_a", "keep_b"
        for name, value in zip(names, weight_grad_blocks(v["index"], near(t), grads(), wanted)):
            v[name + str(t)] = value

    def spread(t):
        v["a%d" % t], v["b%d" % t], v["ab%d" % t] = join(*(v[n + str(t)] for n in ("da", "db", "ga", "gb")))

    def finish(t, early, late):
        pieces = []
        if early:
            for name, other in (("ab%d", False), ("ab%d_c", True)):
                array = v[name % t]
                pieces += [(array, 0, other, 0, (0, 3)), (array, half, other, 1, (0, 1))]
        if late:
            for name, other in (("l%s%d", False), ("l%s%d_c", True)):
                pieces += [(v[name % ("a", t)], 0, other, 0, (1, 2)), (v[name % ("b", t)], 0, other, 1, (3, 2))]
        v["weight_grad"] = place(v["index"], pieces, ROW_CHUNKS[t][0], width, cols, v.here.get("weight_grad"))

    v["theirs"], v["mine"], v["index"] = prepare(features, cotangent)
    v.end()

    v.send("away", "mine", SECTION, "section")
    v.send("rows", "theirs", CORE)
    v.send("mine_c", "mine", CORE)
    v.land("rows")
    v["n0"], v["n1"] = normalize(v["index"], features, v["rows"], layer_norm_gain, layer_norm_bias)
    v.land("mine_c")
    v.end("theirs")

    for k in (1, 3, 2):
        v.send("x0%d" % k, "n0", shift(-k), "tensor")
    v.land("x01", "x03", "x02", "away")
    v.end()

    v.send("away_c", "away", CORE)
    v.land("away_c")
    v.end()

    v.send("x11", "n1", shift(-1), "tensor")
    v.send("x13", "n1", shift(-3), "tensor")
    products(0)
    v.land("x11", "x13")
    v.end()

    v.send("got_a0", "send_a0", Y1)
    v.send("got_b0", "send_b0", Y3)
    v.send("x12", "n1", shift(-2), "tensor")
    for k, part in zip((0, 1, 3, 2), row_gradients(v["index"], grads(), proj_weight)):
        v["r%d" % k] = part
    v.land("got_a0", "got_b0", "x12")
    v.end("send_a0", "send_b0")

    v["n_a0"], v["n_b0"] = add_first(v["next_a0"], v["next_b0"], v["got_a0"], v["got_b0"])
    v.end("next_a0", "next_b0")

    v.send("more_a0", "n_a0", Y3)
    v.send("more_b0", "n_b0", Y1)
    products(1)
    v.land("more_a0", "more_b0")
    v.end("n_a0", "n_b0", "mine", "away", "mine_c", "away_c")

    v["keep0"] = add_second(*(v[n + "0"] for n in ("keep_a", "keep_b", "got_a", "got_b", "more_a", "more_b")))
    v.end("keep_a0", "keep_b0", "got_a0", "got_b0", "more_a0", "more_b0")

    v.send("got_a1", "send_a1", Y1)
    v.send("got_b1", "send_b1", Y3)
    v.send("other0", "keep0", ZLO)
    v.send("s2", "r2", shift(2), "tensor")
    v["own"], v["other"] = project(v["index"], [near(0), near(1)], proj_weight)
    v.land("got_a1", "got_b1", "other0", "s2")
    v.end("r2", "send_a1", "send_b1", "x01", "x03", "x02", "x11", "x13", "x12", "n0", "n1")

    v["n_a1"], v["n_b1"] = add_first(v["next_a1"], v["next_b1"], v["got_a1"], v["got_b1"])
    v["da0"], v["db0"] = add_third(v["keep0"], v["other0"])
    v.end("next_a1", "next_b1", "keep0", "other0")

    v.send("more_a1", "n_a1", Y3)
    v.send("more_b1", "n_b1", Y1)
    v.send("ga0", "da0", Y3)
    v.send("gb0", "db0", Y1)
    v.send("other_c", "other", CORE)
    v.land("more_a1", "more_b1", "ga0", "gb0", "other_c")
    v.end("n_a1", "n_b1", "other")

    v["keep1"] = add_second(*(v[n + "1"] for n in ("keep_a", "keep_b", "got_a", "got_b", "more_a", "more_b")))
    spread(0)
    v.end("keep_a1", "keep_b1", "got_a1", "got_b1", "more_a1", "more_b1", "da0", "db0", "ga0", "gb0")

    v.send("other1", "keep1", ZLO)
    v.send("la0", "a0", Y1)
    v.send("lb0", "b0", Y3)
    v.send("s1", "r1", shift(1), "tensor")
    v.send("s3", "r3", shift(3), "tensor")
    rows = [slice(128 * n, 128 * (n + 1)) for n in range(4)]
    v["up0"], v["up1"] = sums(*([(v["own"], (r, EVERY)), (v["other_c"], (r, EVERY))] for r in rows[2:]))
    v.land("other1", "la0", "lb0", "s1", "s3")
    v.end("a0", "b0", "r1", "r3")

    v["da1"], v["db1"] = add_third(v["keep1"], v["other1"])
    v.end("keep1", "other1")

    v.send("ga1", "da1", Y3)
    v.send("gb1", "db1", Y1)
    v.send("back0", "up0", SECTION, "section")
    v.send("ab0_c", "ab0", CORE)
    v.send("la0_c", "la0", CORE)
    hidden = normalize_backward(
        v["index"], features, v["rows"], layer_norm_gain, [v["r0"], v["s1"], v["s3"], v["s2"]]
    )
    v["ours"], v["hidden"] = hidden[0], hidden[1]
    v.land("ga1", "gb1", "ab0_c", "la0_c", "back0")
    v.end("up0", "r0", "s1", "s3", "s2")

    spread(1)
    v.end("da1", "db1", "ga1", "gb1")

    v.send("la1", "a1", Y1)
    v.send("lb1", "b1", Y3)
    v.send("ab1_c", "ab1", CORE)
    v.send("back1", "up1", SECTION, "section")
    v.send("lb0_c", "lb0", CORE)
    v.land("lb0_c")
    finish(0, True, True)
    v.land("ab1_c")
    finish(1, True, False)
    v.land("la1", "lb1", "back1")
    v.end("a1", "b1", "ab0", "ab0_c", "ab1", "ab1_c", "la0", "lb0", "la0_c", "lb0_c", "up1")

    v.send("la1_c", "la1", CORE)
    v.send("lb1_c", "lb1", CORE)
    v.send("hidden_c", "hidden", CORE)
    v["projected"] = sums(
        *([(v["own"], (r, EVERY)), (v["other_c"], (r, EVERY)), (v[b], (EVERY, EVERY))] for r, b in zip(rows, ("back0", "back1"))),
        stack=True,
    )[0]
    v.land("la1_c", "lb1_c", "hidden_c")
    v.end("own", "other_c", "back0", "back1", "hidden")
    finish(1, False, True)
    v["result"] = jnp.where(
        v["index"][0] == 0, jnp.stack([v["ours"], v["hidden_c"]]), jnp.stack([v["hidden_c"], v["ours"]])
    )
    return (v["projected"][None], v["weight_grad"], v["result"])


def solution(mesh):
    return jax.shard_map(
        body,
        mesh=mesh,
        in_specs=(
            P("section", ("dp", "tensor"), None),
            P("section", None),
            P("section", None),
            P("section", "tensor"),
            P("dp", "section", "tensor"),
        ),
        out_specs=(
            P("dp", "section", "tensor"),
            P("section", "tensor"),
            P("section", ("dp", "tensor"), None),
        ),
        check_vma=False,
    )
```

```python
import jax
import jax.numpy as jnp
from jax import lax
from jax.experimental import pallas as pl
from jax.experimental.pallas import tpu as pltpu
from jax.sharding import PartitionSpec as P

F32 = jnp.float32
BF16 = jnp.bfloat16
VMEM_LIMIT = 20 * 1024 * 1024

ROW_CHUNKS = ((0, 640), (640, 640))


def dp_pairs(fy=lambda y: y, fz=lambda z: z, fc=lambda c: c):
    return [(i, fy(i // 4) * 4 + fz(i // 2 % 2) * 2 + fc(i % 2)) for i in range(16)]


Y1 = dp_pairs(fy=lambda y: y ^ 1)
Y3 = dp_pairs(fy=lambda y: y ^ 3)
ZLO = dp_pairs(fz=lambda z: z ^ 1)
CORE = dp_pairs(fc=lambda c: c ^ 1)
SECTION = [(0, 1), (1, 0)]
AROUND, SLOT_OF, SLOTS = 1, 5, 9


def shift(step):
    return [(i, (i + step) % 4) for i in range(4)]


def swap(value, pairs, axis="dp"):
    return lax.ppermute(value, axis, pairs)


ANY = pl.BlockSpec(memory_space=pl.ANY)
VMEM = pl.BlockSpec(memory_space=pltpu.VMEM)
SMEM = pl.BlockSpec(memory_space=pltpu.SMEM)


class Copies:
    def __init__(self, sems):
        self.sems, self.all = sems, []

    def start(self, *pairs):
        copies = []
        for source, target in pairs:
            copies.append(pltpu.make_async_copy(source, target, self.sems.at[len(self.all)]))
            copies[-1].start()
            self.all.append(copies[-1])
        return copies


def wait(*groups):
    for group in groups:
        for copy in group:
            copy.wait()


def call(kernel, operands, in_specs, out_shapes, out_specs, scratch=(), aliases=None):
    return pl.pallas_call(
        kernel,
        in_specs=in_specs,
        out_specs=out_specs,
        out_shape=out_shapes,
        scratch_shapes=scratch,
        input_output_aliases=aliases or {},
        compiler_params=pltpu.CompilerParams(vmem_limit_bytes=VMEM_LIMIT),
        cost_estimate=pl.CostEstimate(flops=1, bytes_accessed=1, transcendentals=0),
    )(*operands)


def prepare(features, cotangent, gain, bias):
    _, rows, width = features.shape
    _, tokens, cols = cotangent.shape
    part = cols // 4

    def kernel(features, cotangent, gain, bias, ours_out, theirs_out, mine_out, scale_out, index_out, sems):
        s, d, x = lax.axis_index("section"), lax.axis_index("dp"), lax.axis_index("tensor")
        y, c = d // 4, d % 2
        around = (y, y + 1 - 2 * (y % 2), (y + 2) % 4, 3 - y)
        copies = Copies(sems)
        copies.start((features.at[c], ours_out), (features.at[1 - c], theirs_out))
        for n, j in enumerate(around):
            at = pl.ds(pl.multiple_of(j * part, part), part)
            copies.start((cotangent.at[0, :, at], mine_out.at[:, n * part : (n + 1) * part]))
        index_out[0] = c
        for n, j in enumerate(around):
            index_out[AROUND + n] = j
        for t in range(4):
            index_out[SLOT_OF + t] = (s if t < 2 else 1 - s) * 2 + t % 2
        for n, t in enumerate((x, (x + 1) % 4, (x + 3) % 4, (x + 2) % 4)):
            index_out[SLOTS + n] = ((t // 2 + s) % 2) * 2 + t % 2
        scale_out[0:1] = gain[pl.ds(c, 1)]
        scale_out[1:2] = bias[pl.ds(c, 1)]
        wait(copies.all)

    return call(
        kernel,
        [features, cotangent, gain, bias],
        [ANY, ANY, VMEM, VMEM],
        [out(rows, width), out(rows, width), out(tokens, cols), out(2, width, dtype=F32), out(13, dtype=jnp.int32)],
        [VMEM, VMEM, VMEM, VMEM, SMEM],
        [pltpu.SemaphoreType.DMA((6,))],
    )


def sums(*wanted, stack=False):
    arrays = []
    for terms in wanted:
        for array, _ in terms:
            if not any(array is a for a in arrays):
                arrays.append(array)
    places = [[(next(k for k, a in enumerate(arrays) if a is array), at) for array, at in terms] for terms in wanted]
    shapes = [out(*jax.eval_shape(lambda a, at=terms[0][1]: a[at], terms[0][0]).shape) for terms in wanted]
    made = [out(sum(s.shape[0] for s in shapes), *shapes[0].shape[1:])] if stack else shapes
    ends = [sum(s.shape[0] for s in shapes[: n + 1]) for n in range(len(shapes))]

    def kernel(*refs):
        ins, outs = refs[: len(arrays)], refs[len(arrays) :]
        for n, terms in enumerate(places):
            total = None
            for k, at in terms:
                value = ins[k][at].astype(F32)
                total = value if total is None else total + value
            if stack:
                outs[0][ends[n] - shapes[n].shape[0] : ends[n]] = total.astype(BF16)
            else:
                outs[n][...] = total.astype(BF16)

    return call(kernel, arrays, [VMEM] * len(arrays), made, [VMEM] * len(made))


def out(*shape, dtype=BF16):
    return jax.ShapeDtypeStruct(shape, dtype)


def dot(a, b, contract=(1, 0)):
    return lax.dot_general(a, b, (((contract[0],), (contract[1],)), ((), ())), preferred_element_type=F32)


def moments(value):
    mean = jnp.mean(value, axis=-1, keepdims=True)
    centered = value - mean
    inverse = 1.0 / jnp.sqrt(jnp.mean(centered * centered, axis=-1, keepdims=True) + 1e-05)
    return centered * inverse, inverse


def normalize(ours, theirs, scale):
    rows = ours.shape[0]

    def kernel(ours, theirs, scale, *outs):
        gain, bias = scale[0:1], scale[1:2]
        for k, value in enumerate((ours, theirs)):
            standard, _ = moments(value[...].astype(F32))
            normed = (standard * gain + bias).astype(BF16)
            for (start, size), out_ref in zip(ROW_CHUNKS, outs):
                out_ref[k] = normed[:, start : start + size]

    shapes = [out(2, rows, size) for _, size in ROW_CHUNKS]
    return call(kernel, [ours, theirs, scale], [VMEM] * 3, shapes, [VMEM] * len(shapes))


def normalize_backward(ours, theirs, scale, parts):
    count = len(parts)

    def kernel(ours, theirs, scale, *refs):
        gain = scale[0:1]
        for k, value in enumerate((ours, theirs)):
            standard, inverse = moments(value[...].astype(F32))
            total = refs[0][k].astype(F32)
            for ref in refs[1:count]:
                total = total + ref[k].astype(F32)
            scaled = total * gain
            hidden = inverse * (
                scaled
                - jnp.mean(scaled, axis=-1, keepdims=True)
                - standard * jnp.mean(scaled * standard, axis=-1, keepdims=True)
            )
            refs[count + k][...] = hidden.astype(BF16)

    shapes = [out(*ours.shape)] * 2
    return call(kernel, [ours, theirs, scale, *parts], [VMEM] * (3 + count), shapes, [VMEM] * 2)


def both_taps(index, ours, theirs):
    def kernel(index, ours, theirs, result, sems):
        copies = Copies(sems)
        copies.start((ours, result.at[index[0]]), (theirs, result.at[1 - index[0]]))
        wait(copies.all)

    shape = out(2, *ours.shape)
    return call(
        kernel, [index, ours, theirs], [SMEM, VMEM, VMEM], [shape], [ANY], [pltpu.SemaphoreType.DMA((2,))]
    )[0]


def weight_grad_blocks(index, normed, grads, wanted):
    rows = normed[0].shape[-1]
    half = rows // 2
    part = grads[0].shape[1] // 4
    shapes = [out(half, blocks * part) for _, _, blocks in wanted]

    def kernel(index, *refs):
        ins, gs, outs, turned = refs[:4], refs[4:8], refs[8:-1], refs[-1]
        for t in range(4):
            for k in range(2):
                at = pl.multiple_of((4 * k + index[SLOTS + t]) * 128, 128)
                turned[:, pl.ds(at, 128)] = ins[t][k].T
        for (h, first, blocks), out_ref in zip(wanted, outs):
            mine = turned[h * half : (h + 1) * half]
            total = None
            for p in range(4):
                term = dot(mine[:, 256 * p : 256 * (p + 1)], gs[p][:, first * part : (first + blocks) * part])
                total = term if total is None else total + term
            out_ref[...] = total.astype(BF16)

    return call(
        kernel,
        [index, *normed, *grads],
        [SMEM] + [VMEM] * 8,
        shapes,
        [VMEM] * len(shapes),
        [pltpu.VMEM((rows, 1024), BF16)],
    )


def take_tap(index, proj_weight):
    width, cols = proj_weight.shape[0] // 2, proj_weight.shape[1]
    step = width // 8

    def kernel(index, weight, result, sems):
        copies = Copies(sems)
        for n in range(8):
            rows = pl.ds(pl.multiple_of(index[0] * width + n * step, step), step)
            copies.start((weight.at[rows], result.at[n * step : (n + 1) * step]))
        wait(copies.all)

    return call(
        kernel,
        [index, proj_weight],
        [SMEM, ANY],
        [out(width, cols)],
        [VMEM],
        [pltpu.SemaphoreType.DMA((8,))],
    )[0]


def row_gradients(index, grads, weight):
    width, cols = weight.shape
    part = cols // 4
    tile = 256

    def kernel(index, *refs):
        gs, w, outs, held, acc = refs[:4], refs[4], refs[5:9], refs[9], refs[10]
        for j in range(4):
            at = pl.multiple_of(index[AROUND + j] * part, part)
            for n in range(4):
                held[256 * n : 256 * (n + 1), pl.ds(at, part)] = gs[n][:, j * part : (j + 1) * part]
        for i in range(width // tile):
            here = slice(i * tile, (i + 1) * tile)
            acc[:, here] = dot(held[...], w[here], (1, 1)).astype(BF16)
        for t in range(4):
            for k in range(2):
                at = pl.multiple_of((4 * k + index[SLOTS + t]) * 128, 128)
                outs[t][k] = acc[pl.ds(at, 128)]

    return call(
        kernel,
        [index, *grads, weight],
        [SMEM] + [VMEM] * 5,
        [out(2, 128, width)] * 4,
        [VMEM] * 4,
        [pltpu.VMEM((1024, cols), BF16), pltpu.VMEM((1024, width), BF16)],
    )


def project(index, chunks, weight):
    width, cols = weight.shape
    part = cols // 4
    flat = [piece for chunk in chunks for piece in chunk]
    count = len(flat)

    def kernel(index, *refs):
        ins, w, own, other, held = refs[:count], refs[count], refs[count + 1], refs[count + 2], refs[count + 3]
        for m, (first, size) in enumerate(ROW_CHUNKS):
            for t in range(4):
                for k in range(2):
                    at = pl.multiple_of((4 * k + index[SLOTS + t]) * 128, 128)
                    held[pl.ds(at, 128), first : first + size] = ins[4 * m + t][k]
        for i in range(4):
            here = slice(i * part, (i + 1) * part)
            other[:, here] = dot(held[512:], w[:, here]).astype(BF16)
            own[:, here] = dot(held[:512], w[:, here]).astype(BF16)

    return call(
        kernel,
        [index, *flat, weight],
        [SMEM] + [VMEM] * (count + 1),
        [out(512, cols)] * 2,
        [VMEM] * 2,
        [pltpu.VMEM((1024, width), BF16)],
    )


EVERY = slice(None)


def add_first(next_a, next_b, got_a, got_b):
    part = next_a.shape[1]
    left, right = (EVERY, slice(0, part)), (EVERY, slice(part, 2 * part))
    return sums([(next_a, (EVERY, EVERY)), (got_a, right)], [(next_b, (EVERY, EVERY)), (got_b, left)])


def add_second(keep_a, keep_b, got_a, got_b, more_a, more_b):
    part = keep_a.shape[1]
    whole, left, right = (EVERY, EVERY), (EVERY, slice(0, part)), (EVERY, slice(part, 2 * part))
    return sums(
        [(keep_a, whole), (got_a, left), (more_a, whole)],
        [(keep_b, whole), (got_b, right), (more_b, whole)],
        stack=True,
    )[0]


def add_third(keep, other):
    half = keep.shape[0] // 2
    top, bottom = (slice(0, half), EVERY), (slice(half, 2 * half), EVERY)
    return sums([(keep, top), (other, top)], [(keep, bottom), (other, bottom)])


def join(left_a, left_b, right_a, right_b):
    half, part = left_a.shape

    def kernel(left_a, left_b, right_a, right_b, out_a, out_b, both):
        for n, (left, right, single) in enumerate(((left_a, right_a, out_a), (left_b, right_b, out_b))):
            rows = slice(n * half, (n + 1) * half)
            for source, here in ((left, slice(0, part)), (right, slice(part, 2 * part))):
                value = source[...]
                single[:, here] = value
                both[rows, here] = value

    return call(
        kernel,
        [left_a, left_b, right_a, right_b],
        [VMEM] * 4,
        [out(half, 2 * part), out(half, 2 * part), out(2 * half, 2 * part)],
        [VMEM] * 3,
    )


def below(top, bottom):
    rows = top.shape[0]

    def kernel(top, bottom, both):
        both[:rows] = top[...]
        both[rows:] = bottom[...]

    return call(kernel, [top, bottom], [VMEM] * 2, [out(2 * rows, top.shape[1])], [VMEM])[0]


def place(index, pieces, start, width, cols, into):
    part = cols // 4
    half = next(size for first, size in ROW_CHUNKS if first == start) // 2
    arrays = []
    for piece in pieces:
        if not any(piece[0] is a for a in arrays):
            arrays.append(piece[0])
    which = [next(k for k, a in enumerate(arrays) if a is piece[0]) for piece in pieces]
    count = len(arrays)

    def kernel(index, *refs):
        sources, result, sems = refs[:count], refs[-2], refs[-1]
        copies = Copies(sems)
        for k, (_, row, other, h, js) in zip(which, pieces):
            tap = 1 - index[0] if other else index[0]
            rows = pl.ds(pl.multiple_of(tap * width + start + h * half, 64), half)
            for n, j in enumerate(js):
                at = pl.ds(pl.multiple_of(index[AROUND + j] * part, part), part)
                copies.start((sources[k].at[row : row + half, n * part : (n + 1) * part], result.at[rows, at]))
        wait(copies.all)

    operands = [index, *arrays] + ([] if into is None else [into])
    return call(
        kernel,
        operands,
        [SMEM] + [VMEM] * count + ([] if into is None else [ANY]),
        [out(2 * width, cols)],
        [ANY],
        [pltpu.SemaphoreType.DMA((2 * len(pieces),))],
        {} if into is None else {count + 1: 0},
    )[0]


class Phases:
    def __init__(self):
        self.here, self.away = {}, {}

    def __getitem__(self, name):
        return self.here[name]

    def __setitem__(self, name, value):
        self.here[name] = value

    def send(self, name, source, pairs, axis="dp"):
        self.away[name] = swap(self.here[source], pairs, axis)

    def land(self, *names):
        for name in names:
            self.here[name] = self.away.pop(name)

    def end(self, *drop):
        for name in drop:
            del self.here[name]
        self.here = lax.optimization_barrier(self.here)


def body(features, layer_norm_gain, layer_norm_bias, proj_weight, cotangent):
    width = layer_norm_gain.shape[1]
    cols = proj_weight.shape[1]
    half = ROW_CHUNKS[0][1] // 2
    wanted = ((0, 1, 2), (1, 2, 2), (0, 3, 1), (1, 1, 1), (0, 0, 1), (1, 0, 1))
    v = Phases()

    def near(n):
        return [v["n%d" % n], *(v["x%d%d" % (n, k)] for k in (1, 3, 2))]

    def grads():
        return [v["mine"], v["away"], v["mine_c"], v["away_c"]]

    def products(t):
        names = "send_a", "send_b", "next_a", "next_b", "keep_a", "keep_b"
        for name, value in zip(names, weight_grad_blocks(v["index"], near(t), grads(), wanted)):
            v[name + str(t)] = value

    def spread(t):
        v["a%d" % t], v["b%d" % t], v["ab%d" % t] = join(*(v[n + str(t)] for n in ("da", "db", "ga", "gb")))

    def finish(t, early, late):
        pieces = []
        for arrays, places in ((early, ((0, 3), (0, 1))), (late, ((1, 2), (3, 2)))):
            for n, array in enumerate(arrays):
                if len(arrays) == 2:
                    pieces += [(array, h * half, n == 1, h, places[h]) for h in range(2)]
                else:
                    pieces.append((array, 0, n > 1, n % 2, places[n % 2]))
        v["weight_grad"] = place(v["index"], pieces, ROW_CHUNKS[t][0], width, cols, v.here.get("weight_grad"))

    v["ours"], v["theirs"], v["mine"], v["scale"], v["index"] = prepare(
        features, cotangent, layer_norm_gain, layer_norm_bias
    )
    v.end()

    v.send("away", "mine", SECTION, "section")
    v.send("rows", "theirs", CORE)
    v.send("mine_c", "mine", CORE)
    v.land("rows")
    v["n0"], v["n1"] = normalize(v["ours"], v["rows"], v["scale"])
    v.land("mine_c")
    v.end("theirs")

    for k in (1, 3, 2):
        v.send("x0%d" % k, "n0", shift(-k), "tensor")
    v["weight"] = take_tap(v["index"], proj_weight)
    v.land("x01", "x03", "x02", "away")
    v.end()

    v.send("away_c", "away", CORE)
    v.send("x11", "n1", shift(-1), "tensor")
    v.send("x13", "n1", shift(-3), "tensor")
    v.land("away_c")
    v.end()

    products(0)
    v.land("x11", "x13")
    v.end()

    v.send("got_a0", "send_a0", Y1)
    v.send("got_b0", "send_b0", Y3)
    v.send("x12", "n1", shift(-2), "tensor")
    for k, part in zip((0, 1, 3, 2), row_gradients(v["index"], grads(), v["weight"])):
        v["r%d" % k] = part
    v.land("got_a0", "got_b0", "x12")
    v.end("send_a0", "send_b0")

    v["n_a0"], v["n_b0"] = add_first(v["next_a0"], v["next_b0"], v["got_a0"], v["got_b0"])
    v.end("next_a0", "next_b0")

    v.send("more_a0", "n_a0", Y3)
    v.send("more_b0", "n_b0", Y1)
    products(1)
    v.land("more_a0", "more_b0")
    v.end("n_a0", "n_b0", "mine", "away", "mine_c", "away_c")

    v["keep0"] = add_second(*(v[n + "0"] for n in ("keep_a", "keep_b", "got_a", "got_b", "more_a", "more_b")))
    v.end("keep_a0", "keep_b0", "got_a0", "got_b0", "more_a0", "more_b0")

    v.send("got_a1", "send_a1", Y1)
    v.send("got_b1", "send_b1", Y3)
    v.send("other0", "keep0", ZLO)
    v.send("s2", "r2", shift(2), "tensor")
    v["own"], v["other"] = project(v["index"], [near(0), near(1)], v["weight"])
    v.land("got_a1", "got_b1", "other0", "s2")
    v.end("r2", "send_a1", "send_b1", "x01", "x03", "x02", "x11", "x13", "x12", "n0", "n1")

    v["n_a1"], v["n_b1"] = add_first(v["next_a1"], v["next_b1"], v["got_a1"], v["got_b1"])
    v["da0"], v["db0"] = add_third(v["keep0"], v["other0"])
    v.end("next_a1", "next_b1", "keep0", "other0")

    v.send("more_a1", "n_a1", Y3)
    v.send("more_b1", "n_b1", Y1)
    v.send("ga0", "da0", Y3)
    v.send("gb0", "db0", Y1)
    v.send("other_c", "other", CORE)
    v.land("more_a1", "more_b1", "ga0", "gb0", "other_c")
    v.end("n_a1", "n_b1", "other")

    v["keep1"] = add_second(*(v[n + "1"] for n in ("keep_a", "keep_b", "got_a", "got_b", "more_a", "more_b")))
    spread(0)
    v.end("keep_a1", "keep_b1", "got_a1", "got_b1", "more_a1", "more_b1", "da0", "db0", "ga0", "gb0")

    v.send("other1", "keep1", ZLO)
    v.send("la0", "a0", Y1)
    v.send("lb0", "b0", Y3)
    v.send("s1", "r1", shift(1), "tensor")
    v.send("s3", "r3", shift(3), "tensor")
    rows = [slice(0, 112), slice(112, 256), slice(256, 368), slice(368, 512)]
    v["up0"], v["up1"] = sums(*([(v["own"], (r, EVERY)), (v["other_c"], (r, EVERY))] for r in rows[2:]))
    v.land("other1", "la0", "lb0")
    v.end("a0", "b0", "r1", "r3")

    v["da1"], v["db1"] = add_third(v["keep1"], v["other1"])
    v["lab0"] = below(v["la0"], v["lb0"])
    v.land("s1", "s3")
    v.end("keep1", "other1", "la0", "lb0")

    v.send("ga1", "da1", Y3)
    v.send("gb1", "db1", Y1)
    v.send("back0", "up0", SECTION, "section")
    v.send("ab0_c", "ab0", CORE)
    v.send("lab0_c", "lab0", CORE)
    v["own_rows"], v["hidden"] = normalize_backward(
        v["ours"], v["rows"], v["scale"], [v["r0"], v["s1"], v["s3"], v["s2"]]
    )
    v.land("ga1", "gb1", "ab0_c", "lab0_c", "back0")
    v.end("up0", "r0", "s1", "s3", "s2")

    spread(1)
    v.end("da1", "db1", "ga1", "gb1")

    v.send("la1", "a1", Y1)
    v.send("lb1", "b1", Y3)
    v.send("ab1_c", "ab1", CORE)
    v.send("hidden_c", "hidden", CORE)
    v.send("back1", "up1", SECTION, "section")
    finish(0, [v["ab0"], v["ab0_c"]], [v["lab0"], v["lab0_c"]])
    v.land("ab1_c", "hidden_c")
    finish(1, [v["ab1"], v["ab1_c"]], [])
    v["result"] = both_taps(v["index"], v["own_rows"], v["hidden_c"])
    v.land("la1", "lb1", "back1")
    v.end("a1", "b1", "ab0", "ab0_c", "ab1", "ab1_c", "lab0", "lab0_c", "own_rows", "hidden", "hidden_c", "up1")

    v.send("la1_c", "la1", CORE)
    v.send("lb1_c", "lb1", CORE)
    projected = sums(
        *(
            [(v["own"], (r, EVERY)), (v["other_c"], (r, EVERY)), (v[back], (EVERY, EVERY))]
            for r, back in zip(rows, ("back0", "back1"))
        ),
        stack=True,
    )[0]
    v.land("la1_c", "lb1_c")
    finish(1, [], [v["la1"], v["lb1"], v["la1_c"], v["lb1_c"]])
    return (projected[None], v["weight_grad"], v["result"])


def solution(mesh):
    return jax.shard_map(
        body,
        mesh=mesh,
        in_specs=(
            P("section", ("dp", "tensor"), None),
            P("section", None),
            P("section", None),
            P("section", "tensor"),
            P("dp", "section", "tensor"),
        ),
        out_specs=(
            P("dp", "section", "tensor"),
            P("section", "tensor"),
            P("section", ("dp", "tensor"), None),
        ),
        check_vma=False,
    )
```

```python
import jax
import jax.numpy as jnp
from jax import lax
from jax.experimental import pallas as pl
from jax.experimental.pallas import tpu as pltpu
from jax.sharding import PartitionSpec as P

F32 = jnp.float32
BF16 = jnp.bfloat16
VMEM_LIMIT = 20 * 1024 * 1024

ROW_CHUNKS = ((0, 640), (640, 640))


def dp_pairs(fy=lambda y: y, fz=lambda z: z, fc=lambda c: c):
    return [(i, fy(i // 4) * 4 + fz(i // 2 % 2) * 2 + fc(i % 2)) for i in range(16)]


Y1 = dp_pairs(fy=lambda y: y ^ 1)
Y3 = dp_pairs(fy=lambda y: y ^ 3)
ZLO = dp_pairs(fz=lambda z: z ^ 1)
CORE = dp_pairs(fc=lambda c: c ^ 1)
AROUND, SLOT_OF, SLOTS = 1, 5, 9


def swap(value, pairs):
    return lax.ppermute(value, "dp", pairs)


def along_x(value, step):
    return lax.ppermute(value, "tensor", [(i, (i + step) % 4) for i in range(4)])


def to_section(value):
    return lax.ppermute(value, "section", [(0, 1), (1, 0)])


ANY = pl.BlockSpec(memory_space=pl.ANY)
VMEM = pl.BlockSpec(memory_space=pltpu.VMEM)
SMEM = pl.BlockSpec(memory_space=pltpu.SMEM)


class Copies:
    def __init__(self, sems):
        self.sems, self.all = sems, []

    def start(self, *pairs):
        copies = []
        for source, target in pairs:
            copies.append(pltpu.make_async_copy(source, target, self.sems.at[len(self.all)]))
            copies[-1].start()
            self.all.append(copies[-1])
        return copies


def wait(*groups):
    for group in groups:
        for copy in group:
            copy.wait()


def call(kernel, operands, in_specs, out_shapes, out_specs, scratch=(), aliases=None):
    return pl.pallas_call(
        kernel,
        in_specs=in_specs,
        out_specs=out_specs,
        out_shape=out_shapes,
        scratch_shapes=scratch,
        input_output_aliases=aliases or {},
        compiler_params=pltpu.CompilerParams(vmem_limit_bytes=VMEM_LIMIT),
        cost_estimate=pl.CostEstimate(flops=1, bytes_accessed=1, transcendentals=0),
    )(*operands)


def prepare(features, cotangent, gain, bias):
    _, rows, width = features.shape
    _, tokens, cols = cotangent.shape
    part = cols // 4

    def kernel(features, cotangent, gain, bias, ours_out, theirs_out, mine_out, scale_out, index_out, sems):
        s, d, x = lax.axis_index("section"), lax.axis_index("dp"), lax.axis_index("tensor")
        y, c = d // 4, d % 2
        around = (y, y + 1 - 2 * (y % 2), (y + 2) % 4, 3 - y)
        copies = Copies(sems)
        copies.start((features.at[c], ours_out), (features.at[1 - c], theirs_out))
        for n, j in enumerate(around):
            at = pl.ds(pl.multiple_of(j * part, part), part)
            copies.start((cotangent.at[0, :, at], mine_out.at[:, n * part : (n + 1) * part]))
        index_out[0] = c
        for n, j in enumerate(around):
            index_out[AROUND + n] = j
        for t in range(4):
            index_out[SLOT_OF + t] = (s if t < 2 else 1 - s) * 2 + t % 2
        for n, t in enumerate((x, (x + 1) % 4, (x + 3) % 4, (x + 2) % 4)):
            index_out[SLOTS + n] = ((t // 2 + s) % 2) * 2 + t % 2
        scale_out[0:1] = gain[pl.ds(c, 1)]
        scale_out[1:2] = bias[pl.ds(c, 1)]
        wait(copies.all)

    return call(
        kernel,
        [features, cotangent, gain, bias],
        [ANY, ANY, VMEM, VMEM],
        [out(rows, width), out(rows, width), out(tokens, cols), out(2, width, dtype=F32), out(13, dtype=jnp.int32)],
        [VMEM, VMEM, VMEM, VMEM, SMEM],
        [pltpu.SemaphoreType.DMA((6,))],
    )


def sums(*wanted, stack=False):
    arrays = []
    for terms in wanted:
        for array, _ in terms:
            if not any(array is a for a in arrays):
                arrays.append(array)
    places = [[(next(k for k, a in enumerate(arrays) if a is array), at) for array, at in terms] for terms in wanted]
    shapes = [out(*jax.eval_shape(lambda a, at=terms[0][1]: a[at], terms[0][0]).shape) for terms in wanted]
    made = [out(sum(s.shape[0] for s in shapes), *shapes[0].shape[1:])] if stack else shapes
    ends = [sum(s.shape[0] for s in shapes[: n + 1]) for n in range(len(shapes))]

    def kernel(*refs):
        ins, outs = refs[: len(arrays)], refs[len(arrays) :]
        for n, terms in enumerate(places):
            total = None
            for k, at in terms:
                value = ins[k][at].astype(F32)
                total = value if total is None else total + value
            if stack:
                outs[0][ends[n] - shapes[n].shape[0] : ends[n]] = total.astype(BF16)
            else:
                outs[n][...] = total.astype(BF16)

    return call(kernel, arrays, [VMEM] * len(arrays), made, [VMEM] * len(made))


def out(*shape, dtype=BF16):
    return jax.ShapeDtypeStruct(shape, dtype)


def dot(a, b, contract=(1, 0)):
    return lax.dot_general(a, b, (((contract[0],), (contract[1],)), ((), ())), preferred_element_type=F32)


def moments(value):
    mean = jnp.mean(value, axis=-1, keepdims=True)
    centered = value - mean
    inverse = 1.0 / jnp.sqrt(jnp.mean(centered * centered, axis=-1, keepdims=True) + 1e-05)
    return centered * inverse, inverse


def normalize(ours, theirs, scale):
    rows = ours.shape[0]

    def kernel(ours, theirs, scale, *outs):
        gain, bias = scale[0:1], scale[1:2]
        for k, value in enumerate((ours, theirs)):
            standard, _ = moments(value[...].astype(F32))
            normed = (standard * gain + bias).astype(BF16)
            for (start, size), out_ref in zip(ROW_CHUNKS, outs):
                out_ref[k] = normed[:, start : start + size]

    shapes = [out(2, rows, size) for _, size in ROW_CHUNKS]
    return call(kernel, [ours, theirs, scale], [VMEM] * 3, shapes, [VMEM] * len(shapes))


def normalize_backward(ours, theirs, scale, parts):
    count = len(parts)

    def kernel(ours, theirs, scale, *refs):
        gain = scale[0:1]
        for k, value in enumerate((ours, theirs)):
            standard, inverse = moments(value[...].astype(F32))
            total = refs[0][k].astype(F32)
            for ref in refs[1:count]:
                total = total + ref[k].astype(F32)
            scaled = total * gain
            hidden = inverse * (
                scaled
                - jnp.mean(scaled, axis=-1, keepdims=True)
                - standard * jnp.mean(scaled * standard, axis=-1, keepdims=True)
            )
            refs[count + k][...] = hidden.astype(BF16)

    shapes = [out(*ours.shape)] * 2
    return call(kernel, [ours, theirs, scale, *parts], [VMEM] * (3 + count), shapes, [VMEM] * 2)


def both_taps(index, ours, theirs):
    def kernel(index, ours, theirs, result, sems):
        copies = Copies(sems)
        copies.start((ours, result.at[index[0]]), (theirs, result.at[1 - index[0]]))
        wait(copies.all)

    shape = out(2, *ours.shape)
    return call(
        kernel, [index, ours, theirs], [SMEM, VMEM, VMEM], [shape], [ANY], [pltpu.SemaphoreType.DMA((2,))]
    )[0]


def weight_grad_blocks(index, normed, grads, wanted):
    rows = normed[0].shape[-1]
    half = rows // 2
    part = grads[0].shape[1] // 4
    shapes = [out(half, blocks * part) for _, _, blocks in wanted]

    def kernel(index, *refs):
        ins, gs, outs, turned = refs[:4], refs[4:8], refs[8:-1], refs[-1]
        for t in range(4):
            for k in range(2):
                at = pl.multiple_of((4 * k + index[SLOTS + t]) * 128, 128)
                turned[:, pl.ds(at, 128)] = ins[t][k].T
        for (h, first, blocks), out_ref in zip(wanted, outs):
            mine = turned[h * half : (h + 1) * half]
            total = None
            for p in range(4):
                term = dot(mine[:, 256 * p : 256 * (p + 1)], gs[p][:, first * part : (first + blocks) * part])
                total = term if total is None else total + term
            out_ref[...] = total.astype(BF16)

    return call(
        kernel,
        [index, *normed, *grads],
        [SMEM] + [VMEM] * 8,
        shapes,
        [VMEM] * len(shapes),
        [pltpu.VMEM((rows, 1024), BF16)],
    )


def take_tap(index, proj_weight):
    width, cols = proj_weight.shape[0] // 2, proj_weight.shape[1]
    step = width // 8

    def kernel(index, weight, result, sems):
        copies = Copies(sems)
        for n in range(8):
            rows = pl.ds(pl.multiple_of(index[0] * width + n * step, step), step)
            copies.start((weight.at[rows], result.at[n * step : (n + 1) * step]))
        wait(copies.all)

    return call(
        kernel,
        [index, proj_weight],
        [SMEM, ANY],
        [out(width, cols)],
        [VMEM],
        [pltpu.SemaphoreType.DMA((8,))],
    )[0]


def row_gradients(index, grads, weight):
    width, cols = weight.shape
    part = cols // 4
    tile = 256

    def kernel(index, *refs):
        gs, w, outs, held, acc = refs[:4], refs[4], refs[5:9], refs[9], refs[10]
        for j in range(4):
            at = pl.multiple_of(index[AROUND + j] * part, part)
            for n in range(4):
                held[256 * n : 256 * (n + 1), pl.ds(at, part)] = gs[n][:, j * part : (j + 1) * part]
        for i in range(width // tile):
            here = slice(i * tile, (i + 1) * tile)
            acc[:, here] = dot(held[...], w[here], (1, 1)).astype(BF16)
        for t in range(4):
            for k in range(2):
                at = pl.multiple_of((4 * k + index[SLOTS + t]) * 128, 128)
                outs[t][k] = acc[pl.ds(at, 128)]

    return call(
        kernel,
        [index, *grads, weight],
        [SMEM] + [VMEM] * 5,
        [out(2, 128, width)] * 4,
        [VMEM] * 4,
        [pltpu.VMEM((1024, cols), BF16), pltpu.VMEM((1024, width), BF16)],
    )


def project(index, chunks, weight):
    width, cols = weight.shape
    part = cols // 4
    flat = [piece for chunk in chunks for piece in chunk]
    count = len(flat)

    def kernel(index, *refs):
        ins, w, own, other, held = refs[:count], refs[count], refs[count + 1], refs[count + 2], refs[count + 3]
        for m, (first, size) in enumerate(ROW_CHUNKS):
            for t in range(4):
                for k in range(2):
                    at = pl.multiple_of((4 * k + index[SLOTS + t]) * 128, 128)
                    held[pl.ds(at, 128), first : first + size] = ins[4 * m + t][k]
        for i in range(4):
            here = slice(i * part, (i + 1) * part)
            other[:, here] = dot(held[512:], w[:, here]).astype(BF16)
            own[:, here] = dot(held[:512], w[:, here]).astype(BF16)

    return call(
        kernel,
        [index, *flat, weight],
        [SMEM] + [VMEM] * (count + 1),
        [out(512, cols)] * 2,
        [VMEM] * 2,
        [pltpu.VMEM((1024, width), BF16)],
    )


EVERY = slice(None)


def add_first(next_a, next_b, got_a, got_b):
    part = next_a.shape[1]
    left, right = (EVERY, slice(0, part)), (EVERY, slice(part, 2 * part))
    return sums([(next_a, (EVERY, EVERY)), (got_a, right)], [(next_b, (EVERY, EVERY)), (got_b, left)])


def add_second(keep_a, keep_b, got_a, got_b, more_a, more_b):
    part = keep_a.shape[1]
    whole, left, right = (EVERY, EVERY), (EVERY, slice(0, part)), (EVERY, slice(part, 2 * part))
    return sums(
        [(keep_a, whole), (got_a, left), (more_a, whole)],
        [(keep_b, whole), (got_b, right), (more_b, whole)],
        stack=True,
    )[0]


def add_third(keep, other):
    half = keep.shape[0] // 2
    top, bottom = (slice(0, half), EVERY), (slice(half, 2 * half), EVERY)
    return sums([(keep, top), (other, top)], [(keep, bottom), (other, bottom)])


def join(left_a, left_b, right_a, right_b):
    half, part = left_a.shape

    def kernel(left_a, left_b, right_a, right_b, out_a, out_b, both):
        for n, (left, right, single) in enumerate(((left_a, right_a, out_a), (left_b, right_b, out_b))):
            rows = slice(n * half, (n + 1) * half)
            for source, here in ((left, slice(0, part)), (right, slice(part, 2 * part))):
                value = source[...]
                single[:, here] = value
                both[rows, here] = value

    return call(
        kernel,
        [left_a, left_b, right_a, right_b],
        [VMEM] * 4,
        [out(half, 2 * part), out(half, 2 * part), out(2 * half, 2 * part)],
        [VMEM] * 3,
    )


def below(top, bottom):
    rows = top.shape[0]

    def kernel(top, bottom, both):
        both[:rows] = top[...]
        both[rows:] = bottom[...]

    return call(kernel, [top, bottom], [VMEM] * 2, [out(2 * rows, top.shape[1])], [VMEM])[0]


def place(index, pieces, start, width, cols, into):
    part = cols // 4
    half = next(size for first, size in ROW_CHUNKS if first == start) // 2
    arrays = []
    for piece in pieces:
        if not any(piece[0] is a for a in arrays):
            arrays.append(piece[0])
    which = [next(k for k, a in enumerate(arrays) if a is piece[0]) for piece in pieces]
    count = len(arrays)

    def kernel(index, *refs):
        sources, result, sems = refs[:count], refs[-2], refs[-1]
        copies = Copies(sems)
        for k, (_, row, other, h, js) in zip(which, pieces):
            tap = 1 - index[0] if other else index[0]
            rows = pl.ds(pl.multiple_of(tap * width + start + h * half, 64), half)
            for n, j in enumerate(js):
                at = pl.ds(pl.multiple_of(index[AROUND + j] * part, part), part)
                copies.start((sources[k].at[row : row + half, n * part : (n + 1) * part], result.at[rows, at]))
        wait(copies.all)

    operands = [index, *arrays] + ([] if into is None else [into])
    return call(
        kernel,
        operands,
        [SMEM] + [VMEM] * count + ([] if into is None else [ANY]),
        [out(2 * width, cols)],
        [ANY],
        [pltpu.SemaphoreType.DMA((2 * len(pieces),))],
        {} if into is None else {count + 1: 0},
    )[0]


class Phases:
    def end(self):
        self.__dict__ = lax.optimization_barrier(self.__dict__)


def body(features, layer_norm_gain, layer_norm_bias, proj_weight, cotangent):
    width = layer_norm_gain.shape[1]
    cols = proj_weight.shape[1]
    half = ROW_CHUNKS[0][1] // 2
    wanted = ((0, 1, 2), (1, 2, 2), (0, 3, 1), (1, 1, 1), (0, 0, 1), (1, 0, 1))
    v = Phases()

    def grads():
        return [v.mine, v.away, v.mine_c, v.away_c]

    def finish(t, early, late, into):
        pieces = []
        for arrays, places in ((early, ((0, 3), (0, 1))), (late, ((1, 2), (3, 2)))):
            for n, array in enumerate(arrays):
                if len(arrays) == 2:
                    pieces += [(array, h * half, n == 1, h, places[h]) for h in range(2)]
                else:
                    pieces.append((array, 0, n > 1, n % 2, places[n % 2]))
        return place(v.index, pieces, ROW_CHUNKS[t][0], width, cols, into)

    v.ours, v.theirs, v.mine, v.scale, v.index = prepare(
        features, cotangent, layer_norm_gain, layer_norm_bias
    )
    v.end()

    away = to_section(v.mine)
    rows = swap(v.theirs, CORE)
    mine_c = swap(v.mine, CORE)
    v.rows = rows
    v.n0, v.n1 = normalize(v.ours, v.rows, v.scale)
    v.mine_c = mine_c
    del v.theirs
    v.end()

    x01 = along_x(v.n0, -1)
    x03 = along_x(v.n0, -3)
    x02 = along_x(v.n0, -2)
    v.weight = take_tap(v.index, proj_weight)
    v.x01, v.x03, v.x02, v.away = x01, x03, x02, away
    v.end()

    away_c = swap(v.away, CORE)
    x11 = along_x(v.n1, -1)
    x13 = along_x(v.n1, -3)
    v.away_c = away_c
    v.end()

    near0 = [v.n0, v.x01, v.x03, v.x02]
    v.send_a0, v.send_b0, v.next_a0, v.next_b0, v.keep_a0, v.keep_b0 = weight_grad_blocks(
        v.index, near0, grads(), wanted
    )
    v.x11, v.x13 = x11, x13
    v.end()

    got_a0 = swap(v.send_a0, Y1)
    got_b0 = swap(v.send_b0, Y3)
    x12 = along_x(v.n1, -2)
    v.r0, v.r1, v.r3, v.r2 = row_gradients(v.index, grads(), v.weight)
    v.got_a0, v.got_b0, v.x12 = got_a0, got_b0, x12
    del v.send_a0, v.send_b0
    v.end()

    v.n_a0, v.n_b0 = add_first(v.next_a0, v.next_b0, v.got_a0, v.got_b0)
    del v.next_a0, v.next_b0
    v.end()

    more_a0 = swap(v.n_a0, Y3)
    more_b0 = swap(v.n_b0, Y1)
    near1 = [v.n1, v.x11, v.x13, v.x12]
    v.send_a1, v.send_b1, v.next_a1, v.next_b1, v.keep_a1, v.keep_b1 = weight_grad_blocks(
        v.index, near1, grads(), wanted
    )
    v.more_a0, v.more_b0 = more_a0, more_b0
    del v.n_a0, v.n_b0, v.mine, v.away, v.mine_c, v.away_c
    v.end()

    v.keep0 = add_second(
        v.keep_a0, v.keep_b0, v.got_a0, v.got_b0, v.more_a0, v.more_b0
    )
    del v.keep_a0, v.keep_b0, v.got_a0, v.got_b0, v.more_a0, v.more_b0
    v.end()

    got_a1 = swap(v.send_a1, Y1)
    got_b1 = swap(v.send_b1, Y3)
    other0 = swap(v.keep0, ZLO)
    s2 = along_x(v.r2, 2)
    v.own, v.other = project(v.index, [[v.n0, v.x01, v.x03, v.x02], [v.n1, v.x11, v.x13, v.x12]], v.weight)
    v.got_a1, v.got_b1, v.other0, v.s2 = got_a1, got_b1, other0, s2
    del v.r2, v.send_a1, v.send_b1, v.x01, v.x03, v.x02, v.x11, v.x13, v.x12, v.n0, v.n1
    v.end()

    v.n_a1, v.n_b1 = add_first(v.next_a1, v.next_b1, v.got_a1, v.got_b1)
    v.da0, v.db0 = add_third(v.keep0, v.other0)
    del v.next_a1, v.next_b1, v.keep0, v.other0
    v.end()

    more_a1 = swap(v.n_a1, Y3)
    more_b1 = swap(v.n_b1, Y1)
    ga0 = swap(v.da0, Y3)
    gb0 = swap(v.db0, Y1)
    other_c = swap(v.other, CORE)
    v.more_a1, v.more_b1, v.ga0, v.gb0, v.other_c = more_a1, more_b1, ga0, gb0, other_c
    del v.n_a1, v.n_b1, v.other
    v.end()

    v.keep1 = add_second(
        v.keep_a1, v.keep_b1, v.got_a1, v.got_b1, v.more_a1, v.more_b1
    )
    v.a0, v.b0, v.ab0 = join(v.da0, v.db0, v.ga0, v.gb0)
    del v.keep_a1, v.keep_b1, v.got_a1, v.got_b1, v.more_a1, v.more_b1, v.da0, v.db0, v.ga0, v.gb0
    v.end()

    other1 = swap(v.keep1, ZLO)
    la0 = swap(v.a0, Y1)
    lb0 = swap(v.b0, Y3)
    s1 = along_x(v.r1, 1)
    s3 = along_x(v.r3, 3)
    rows = [slice(0, 112), slice(112, 256), slice(256, 368), slice(368, 512)]
    v.up0, v.up1 = sums(*([(v.own, (r, EVERY)), (v.other_c, (r, EVERY))] for r in rows[2:]))
    v.other1, v.la0, v.lb0 = other1, la0, lb0
    del v.a0, v.b0, v.r1, v.r3
    v.end()

    v.da1, v.db1 = add_third(v.keep1, v.other1)
    v.lab0 = below(v.la0, v.lb0)
    v.s1, v.s3 = s1, s3
    del v.keep1, v.other1, v.la0, v.lb0
    v.end()

    ga1 = swap(v.da1, Y3)
    gb1 = swap(v.db1, Y1)
    back0 = to_section(v.up0)
    ab0_c = swap(v.ab0, CORE)
    lab0_c = swap(v.lab0, CORE)
    v.own_rows, v.hidden = normalize_backward(
        v.ours, v.rows, v.scale, [v.r0, v.s1, v.s3, v.s2]
    )
    v.ga1, v.gb1, v.ab0_c, v.lab0_c, v.back0 = ga1, gb1, ab0_c, lab0_c, back0
    del v.up0, v.r0, v.s1, v.s3, v.s2
    v.end()

    v.a1, v.b1, v.ab1 = join(v.da1, v.db1, v.ga1, v.gb1)
    del v.da1, v.db1, v.ga1, v.gb1
    v.end()

    la1 = swap(v.a1, Y1)
    lb1 = swap(v.b1, Y3)
    ab1_c = swap(v.ab1, CORE)
    hidden_c = swap(v.hidden, CORE)
    back1 = to_section(v.up1)
    v.weight_grad = finish(0, [v.ab0, v.ab0_c], [v.lab0, v.lab0_c], None)
    v.ab1_c, v.hidden_c = ab1_c, hidden_c
    v.weight_grad = finish(1, [v.ab1, v.ab1_c], [], v.weight_grad)
    v.result = both_taps(v.index, v.own_rows, v.hidden_c)
    v.la1, v.lb1, v.back1 = la1, lb1, back1
    del v.a1, v.b1, v.ab0, v.ab0_c, v.ab1, v.ab1_c, v.lab0, v.lab0_c, v.own_rows, v.hidden, v.hidden_c, v.up1
    v.end()

    la1_c = swap(v.la1, CORE)
    lb1_c = swap(v.lb1, CORE)
    projected = sums(
        *(
            [(v.own, (r, EVERY)), (v.other_c, (r, EVERY)), (back, (EVERY, EVERY))]
            for r, back in zip(rows, (v.back0, v.back1))
        ),
        stack=True,
    )[0]
    v.la1_c, v.lb1_c = la1_c, lb1_c
    v.weight_grad = finish(1, [], [v.la1, v.lb1, v.la1_c, v.lb1_c], v.weight_grad)
    return (projected[None], v.weight_grad, v.result)


def solution(mesh):
    return jax.shard_map(
        body,
        mesh=mesh,
        in_specs=(
            P("section", ("dp", "tensor"), None),
            P("section", None),
            P("section", None),
            P("section", "tensor"),
            P("dp", "section", "tensor"),
        ),
        out_specs=(
            P("dp", "section", "tensor"),
            P("section", "tensor"),
            P("section", ("dp", "tensor"), None),
        ),
        check_vma=False,
    )
```

```python
import jax
import jax.numpy as jnp
from jax import lax
from jax.experimental import pallas as pl
from jax.experimental.pallas import tpu as pltpu
from jax.sharding import PartitionSpec as P

F32 = jnp.float32
BF16 = jnp.bfloat16
VMEM_LIMIT = 20 * 1024 * 1024

ROW_CHUNKS = ((0, 640), (640, 640))


def dp_pairs(fy=lambda y: y, fz=lambda z: z, fc=lambda c: c):
    return [(i, fy(i // 4) * 4 + fz(i // 2 % 2) * 2 + fc(i % 2)) for i in range(16)]


Y1 = dp_pairs(fy=lambda y: y ^ 1)
Y3 = dp_pairs(fy=lambda y: y ^ 3)
ZLO = dp_pairs(fz=lambda z: z ^ 1)
CORE = dp_pairs(fc=lambda c: c ^ 1)
AROUND, SLOT_OF, SLOTS = 1, 5, 9


def swap(value, pairs):
    return lax.ppermute(value, "dp", pairs)


def along_x(value, step):
    return lax.ppermute(value, "tensor", [(i, (i + step) % 4) for i in range(4)])


def to_section(value):
    return lax.ppermute(value, "section", [(0, 1), (1, 0)])


ANY = pl.BlockSpec(memory_space=pl.ANY)
VMEM = pl.BlockSpec(memory_space=pltpu.VMEM)
SMEM = pl.BlockSpec(memory_space=pltpu.SMEM)


class Copies:
    def __init__(self, sems):
        self.sems, self.all = sems, []

    def start(self, *pairs):
        copies = []
        for source, target in pairs:
            copies.append(pltpu.make_async_copy(source, target, self.sems.at[len(self.all)]))
            copies[-1].start()
            self.all.append(copies[-1])
        return copies


def wait(*groups):
    for group in groups:
        for copy in group:
            copy.wait()


def call(kernel, operands, in_specs, out_shapes, out_specs, scratch=(), aliases=None):
    return pl.pallas_call(
        kernel,
        in_specs=in_specs,
        out_specs=out_specs,
        out_shape=out_shapes,
        scratch_shapes=scratch,
        input_output_aliases=aliases or {},
        compiler_params=pltpu.CompilerParams(vmem_limit_bytes=VMEM_LIMIT),
        cost_estimate=pl.CostEstimate(flops=1, bytes_accessed=1, transcendentals=0),
    )(*operands)


def prepare(features, cotangent):
    _, rows, width = features.shape
    _, tokens, cols = cotangent.shape
    part = cols // 4

    def kernel(features, cotangent, ours_out, theirs_out, mine_out, index_out, sems):
        s, d, x = lax.axis_index("section"), lax.axis_index("dp"), lax.axis_index("tensor")
        y, c = d // 4, d % 2
        around = (y, y + 1 - 2 * (y % 2), (y + 2) % 4, 3 - y)
        copies = Copies(sems)
        copies.start((features.at[c], ours_out), (features.at[1 - c], theirs_out))
        for n, j in enumerate(around):
            at = pl.ds(pl.multiple_of(j * part, part), part)
            copies.start((cotangent.at[0, :, at], mine_out.at[:, n * part : (n + 1) * part]))
        index_out[0] = c
        for n, j in enumerate(around):
            index_out[AROUND + n] = j
        for t in range(4):
            index_out[SLOT_OF + t] = (s if t < 2 else 1 - s) * 2 + t % 2
        for n, t in enumerate((x, (x + 1) % 4, (x + 3) % 4, (x + 2) % 4)):
            index_out[SLOTS + n] = ((t // 2 + s) % 2) * 2 + t % 2
        wait(copies.all)

    return call(
        kernel,
        [features, cotangent],
        [ANY, ANY],
        [out(rows, width), out(rows, width), out(tokens, cols), out(13, dtype=jnp.int32)],
        [VMEM, VMEM, VMEM, SMEM],
        [pltpu.SemaphoreType.DMA((6,))],
    )


def sums(*wanted, stack=False):
    arrays = []
    for terms in wanted:
        for array, _ in terms:
            if not any(array is a for a in arrays):
                arrays.append(array)
    places = [[(next(k for k, a in enumerate(arrays) if a is array), at) for array, at in terms] for terms in wanted]
    shapes = [out(*jax.eval_shape(lambda a, at=terms[0][1]: a[at], terms[0][0]).shape) for terms in wanted]
    made = [out(sum(s.shape[0] for s in shapes), *shapes[0].shape[1:])] if stack else shapes
    ends = [sum(s.shape[0] for s in shapes[: n + 1]) for n in range(len(shapes))]

    def kernel(*refs):
        ins, outs = refs[: len(arrays)], refs[len(arrays) :]
        for n, terms in enumerate(places):
            total = None
            for k, at in terms:
                value = ins[k][at].astype(F32)
                total = value if total is None else total + value
            if stack:
                outs[0][ends[n] - shapes[n].shape[0] : ends[n]] = total.astype(BF16)
            else:
                outs[n][...] = total.astype(BF16)

    return call(kernel, arrays, [VMEM] * len(arrays), made, [VMEM] * len(made))


def out(*shape, dtype=BF16):
    return jax.ShapeDtypeStruct(shape, dtype)


def dot(a, b, contract=(1, 0)):
    return lax.dot_general(a, b, (((contract[0],), (contract[1],)), ((), ())), preferred_element_type=F32)


def moments(value):
    mean = jnp.mean(value, axis=-1, keepdims=True)
    centered = value - mean
    inverse = 1.0 / jnp.sqrt(jnp.mean(centered * centered, axis=-1, keepdims=True) + 1e-05)
    return centered * inverse, inverse


def normalize(index, ours, theirs, gain, bias):
    rows = ours.shape[0]

    def kernel(index, ours, theirs, gain, bias, *outs):
        gain, bias = gain[pl.ds(index[0], 1)], bias[pl.ds(index[0], 1)]
        for k, value in enumerate((ours, theirs)):
            standard, _ = moments(value[...].astype(F32))
            normed = (standard * gain + bias).astype(BF16)
            for (start, size), out_ref in zip(ROW_CHUNKS, outs):
                out_ref[k] = normed[:, start : start + size]

    shapes = [out(2, rows, size) for _, size in ROW_CHUNKS]
    return call(kernel, [index, ours, theirs, gain, bias], [SMEM] + [VMEM] * 4, shapes, [VMEM] * len(shapes))


def normalize_backward(index, ours, theirs, gain, parts):
    count = len(parts)

    def kernel(index, ours, theirs, gain, *refs):
        gain = gain[pl.ds(index[0], 1)]
        for k, value in enumerate((ours, theirs)):
            standard, inverse = moments(value[...].astype(F32))
            total = refs[0][k].astype(F32)
            for ref in refs[1:count]:
                total = total + ref[k].astype(F32)
            scaled = total * gain
            hidden = inverse * (
                scaled
                - jnp.mean(scaled, axis=-1, keepdims=True)
                - standard * jnp.mean(scaled * standard, axis=-1, keepdims=True)
            )
            refs[count + k][...] = hidden.astype(BF16)

    shapes = [out(*ours.shape)] * 2
    return call(kernel, [index, ours, theirs, gain, *parts], [SMEM] + [VMEM] * (3 + count), shapes, [VMEM] * 2)


def both_taps(index, ours, theirs):
    def kernel(index, ours, theirs, result, sems):
        copies = Copies(sems)
        copies.start((ours, result.at[index[0]]), (theirs, result.at[1 - index[0]]))
        wait(copies.all)

    shape = out(2, *ours.shape)
    return call(
        kernel, [index, ours, theirs], [SMEM, VMEM, VMEM], [shape], [ANY], [pltpu.SemaphoreType.DMA((2,))]
    )[0]


def weight_grad_blocks(index, normed, grads, wanted):
    rows = normed[0].shape[-1]
    half = rows // 2
    part = grads[0].shape[1] // 4
    shapes = [out(half, blocks * part) for _, _, blocks in wanted]

    def kernel(index, *refs):
        ins, gs, outs, turned = refs[:4], refs[4:8], refs[8:-1], refs[-1]
        for t in range(4):
            for k in range(2):
                at = pl.multiple_of((4 * k + index[SLOTS + t]) * 128, 128)
                turned[:, pl.ds(at, 128)] = ins[t][k].T
        for (h, first, blocks), out_ref in zip(wanted, outs):
            mine = turned[h * half : (h + 1) * half]
            total = None
            for p in range(4):
                term = dot(mine[:, 256 * p : 256 * (p + 1)], gs[p][:, first * part : (first + blocks) * part])
                total = term if total is None else total + term
            out_ref[...] = total.astype(BF16)

    return call(
        kernel,
        [index, *normed, *grads],
        [SMEM] + [VMEM] * 8,
        shapes,
        [VMEM] * len(shapes),
        [pltpu.VMEM((rows, 1024), BF16)],
    )


def take_tap(index, proj_weight):
    width, cols = proj_weight.shape[0] // 2, proj_weight.shape[1]
    step = width // 8

    def kernel(index, weight, result, sems):
        copies = Copies(sems)
        for n in range(8):
            rows = pl.ds(pl.multiple_of(index[0] * width + n * step, step), step)
            copies.start((weight.at[rows], result.at[n * step : (n + 1) * step]))
        wait(copies.all)

    return call(
        kernel,
        [index, proj_weight],
        [SMEM, ANY],
        [out(width, cols)],
        [VMEM],
        [pltpu.SemaphoreType.DMA((8,))],
    )[0]


def row_gradients(index, grads, weight):
    width, cols = weight.shape
    part = cols // 4
    tile = 256

    def kernel(index, *refs):
        gs, w, outs, held, acc = refs[:4], refs[4], refs[5:9], refs[9], refs[10]
        for j in range(4):
            at = pl.multiple_of(index[AROUND + j] * part, part)
            for n in range(4):
                held[256 * n : 256 * (n + 1), pl.ds(at, part)] = gs[n][:, j * part : (j + 1) * part]
        for i in range(width // tile):
            here = slice(i * tile, (i + 1) * tile)
            acc[:, here] = dot(held[...], w[here], (1, 1)).astype(BF16)
        for t in range(4):
            for k in range(2):
                at = pl.multiple_of((4 * k + index[SLOTS + t]) * 128, 128)
                outs[t][k] = acc[pl.ds(at, 128)]

    return call(
        kernel,
        [index, *grads, weight],
        [SMEM] + [VMEM] * 5,
        [out(2, 128, width)] * 4,
        [VMEM] * 4,
        [pltpu.VMEM((1024, cols), BF16), pltpu.VMEM((1024, width), BF16)],
    )


def project(index, chunks, weight):
    width, cols = weight.shape
    part = cols // 4
    flat = [piece for chunk in chunks for piece in chunk]
    count = len(flat)

    def kernel(index, *refs):
        ins, w, own, other, held = refs[:count], refs[count], refs[count + 1], refs[count + 2], refs[count + 3]
        for m, (first, size) in enumerate(ROW_CHUNKS):
            for t in range(4):
                for k in range(2):
                    at = pl.multiple_of((4 * k + index[SLOTS + t]) * 128, 128)
                    held[pl.ds(at, 128), first : first + size] = ins[4 * m + t][k]
        for i in range(4):
            here = slice(i * part, (i + 1) * part)
            other[:, here] = dot(held[512:], w[:, here]).astype(BF16)
            own[:, here] = dot(held[:512], w[:, here]).astype(BF16)

    return call(
        kernel,
        [index, *flat, weight],
        [SMEM] + [VMEM] * (count + 1),
        [out(512, cols)] * 2,
        [VMEM] * 2,
        [pltpu.VMEM((1024, width), BF16)],
    )


EVERY = slice(None)


def add_first(next_a, next_b, got_a, got_b):
    part = next_a.shape[1]
    left, right = (EVERY, slice(0, part)), (EVERY, slice(part, 2 * part))
    return sums([(next_a, (EVERY, EVERY)), (got_a, right)], [(next_b, (EVERY, EVERY)), (got_b, left)])


def add_second(keep_a, keep_b, got_a, got_b, more_a, more_b):
    part = keep_a.shape[1]
    whole, left, right = (EVERY, EVERY), (EVERY, slice(0, part)), (EVERY, slice(part, 2 * part))
    return sums(
        [(keep_a, whole), (got_a, left), (more_a, whole)],
        [(keep_b, whole), (got_b, right), (more_b, whole)],
        stack=True,
    )[0]


def add_third(keep, other):
    half = keep.shape[0] // 2
    top, bottom = (slice(0, half), EVERY), (slice(half, 2 * half), EVERY)
    return sums([(keep, top), (other, top)], [(keep, bottom), (other, bottom)])


def join(left_a, left_b, right_a, right_b):
    half, part = left_a.shape

    def kernel(left_a, left_b, right_a, right_b, out_a, out_b, both):
        for n, (left, right, single) in enumerate(((left_a, right_a, out_a), (left_b, right_b, out_b))):
            rows = slice(n * half, (n + 1) * half)
            for source, here in ((left, slice(0, part)), (right, slice(part, 2 * part))):
                value = source[...]
                single[:, here] = value
                both[rows, here] = value

    return call(
        kernel,
        [left_a, left_b, right_a, right_b],
        [VMEM] * 4,
        [out(half, 2 * part), out(half, 2 * part), out(2 * half, 2 * part)],
        [VMEM] * 3,
    )


def below(top, bottom):
    rows = top.shape[0]

    def kernel(top, bottom, both):
        both[:rows] = top[...]
        both[rows:] = bottom[...]

    return call(kernel, [top, bottom], [VMEM] * 2, [out(2 * rows, top.shape[1])], [VMEM])[0]


def place(index, pieces, start, width, cols, into):
    part = cols // 4
    half = next(size for first, size in ROW_CHUNKS if first == start) // 2
    arrays = []
    for piece in pieces:
        if not any(piece[0] is a for a in arrays):
            arrays.append(piece[0])
    which = [next(k for k, a in enumerate(arrays) if a is piece[0]) for piece in pieces]
    count = len(arrays)

    def kernel(index, *refs):
        sources, result, sems = refs[:count], refs[-2], refs[-1]
        copies = Copies(sems)
        for k, (_, row, other, h, js) in zip(which, pieces):
            tap = 1 - index[0] if other else index[0]
            rows = pl.ds(pl.multiple_of(tap * width + start + h * half, 64), half)
            for n, j in enumerate(js):
                at = pl.ds(pl.multiple_of(index[AROUND + j] * part, part), part)
                copies.start((sources[k].at[row : row + half, n * part : (n + 1) * part], result.at[rows, at]))
        wait(copies.all)

    operands = [index, *arrays] + ([] if into is None else [into])
    return call(
        kernel,
        operands,
        [SMEM] + [VMEM] * count + ([] if into is None else [ANY]),
        [out(2 * width, cols)],
        [ANY],
        [pltpu.SemaphoreType.DMA((2 * len(pieces),))],
        {} if into is None else {count + 1: 0},
    )[0]


class Phases:
    def end(self):
        self.__dict__ = lax.optimization_barrier(self.__dict__)


def body(features, layer_norm_gain, layer_norm_bias, proj_weight, cotangent):
    width = layer_norm_gain.shape[1]
    cols = proj_weight.shape[1]
    half = ROW_CHUNKS[0][1] // 2
    wanted = ((0, 1, 2), (1, 2, 2), (0, 3, 1), (1, 1, 1), (0, 0, 1), (1, 0, 1))
    v = Phases()

    def grads():
        return [v.mine, v.away, v.mine_c, v.away_c]

    def finish(t, early, late, into):
        pieces = []
        for arrays, places in ((early, ((0, 3), (0, 1))), (late, ((1, 2), (3, 2)))):
            for n, array in enumerate(arrays):
                if len(arrays) == 2:
                    pieces += [(array, h * half, n == 1, h, places[h]) for h in range(2)]
                else:
                    pieces.append((array, 0, n > 1, n % 2, places[n % 2]))
        return place(v.index, pieces, ROW_CHUNKS[t][0], width, cols, into)

    v.ours, v.theirs, v.mine, v.index = prepare(features, cotangent)
    v.end()

    away = to_section(v.mine)
    rows = swap(v.theirs, CORE)
    mine_c = swap(v.mine, CORE)
    v.rows = rows
    v.n0, v.n1 = normalize(v.index, v.ours, v.rows, layer_norm_gain, layer_norm_bias)
    v.mine_c = mine_c
    del v.theirs
    v.end()

    x01 = along_x(v.n0, -1)
    x03 = along_x(v.n0, -3)
    x02 = along_x(v.n0, -2)
    v.weight = take_tap(v.index, proj_weight)
    v.x01, v.x03, v.x02, v.away = x01, x03, x02, away
    v.end()

    away_c = swap(v.away, CORE)
    x12 = along_x(v.n1, -2)
    v.away_c = away_c
    v.end()

    near0 = [v.n0, v.x01, v.x03, v.x02]
    v.send_a0, v.send_b0, v.next_a0, v.next_b0, v.keep_a0, v.keep_b0 = weight_grad_blocks(
        v.index, near0, grads(), wanted
    )
    v.x12 = x12
    v.end()

    got_a0 = swap(v.send_a0, Y1)
    got_b0 = swap(v.send_b0, Y3)
    x11 = along_x(v.n1, -1)
    x13 = along_x(v.n1, -3)
    v.r0, v.r1, v.r3, v.r2 = row_gradients(v.index, grads(), v.weight)
    v.got_a0, v.got_b0, v.x11, v.x13 = got_a0, got_b0, x11, x13
    del v.send_a0, v.send_b0
    v.end()

    v.n_a0, v.n_b0 = add_first(v.next_a0, v.next_b0, v.got_a0, v.got_b0)
    del v.next_a0, v.next_b0
    v.end()

    more_a0 = swap(v.n_a0, Y3)
    more_b0 = swap(v.n_b0, Y1)
    near1 = [v.n1, v.x11, v.x13, v.x12]
    v.send_a1, v.send_b1, v.next_a1, v.next_b1, v.keep_a1, v.keep_b1 = weight_grad_blocks(
        v.index, near1, grads(), wanted
    )
    v.more_a0, v.more_b0 = more_a0, more_b0
    del v.n_a0, v.n_b0, v.mine, v.away, v.mine_c, v.away_c
    v.end()

    v.keep0 = add_second(
        v.keep_a0, v.keep_b0, v.got_a0, v.got_b0, v.more_a0, v.more_b0
    )
    del v.keep_a0, v.keep_b0, v.got_a0, v.got_b0, v.more_a0, v.more_b0
    v.end()

    got_a1 = swap(v.send_a1, Y1)
    got_b1 = swap(v.send_b1, Y3)
    other0 = swap(v.keep0, ZLO)
    s2 = along_x(v.r2, 2)
    v.own, v.other = project(v.index, [[v.n0, v.x01, v.x03, v.x02], [v.n1, v.x11, v.x13, v.x12]], v.weight)
    v.got_a1, v.got_b1, v.other0, v.s2 = got_a1, got_b1, other0, s2
    del v.r2, v.send_a1, v.send_b1, v.x01, v.x03, v.x02, v.x11, v.x13, v.x12, v.n0, v.n1
    v.end()

    v.n_a1, v.n_b1 = add_first(v.next_a1, v.next_b1, v.got_a1, v.got_b1)
    v.da0, v.db0 = add_third(v.keep0, v.other0)
    del v.next_a1, v.next_b1, v.keep0, v.other0
    v.end()

    more_a1 = swap(v.n_a1, Y3)
    more_b1 = swap(v.n_b1, Y1)
    ga0 = swap(v.da0, Y3)
    gb0 = swap(v.db0, Y1)
    other_c = swap(v.other, CORE)
    v.more_a1, v.more_b1, v.ga0, v.gb0, v.other_c = more_a1, more_b1, ga0, gb0, other_c
    del v.n_a1, v.n_b1, v.other
    v.end()

    v.keep1 = add_second(
        v.keep_a1, v.keep_b1, v.got_a1, v.got_b1, v.more_a1, v.more_b1
    )
    v.a0, v.b0, v.ab0 = join(v.da0, v.db0, v.ga0, v.gb0)
    del v.keep_a1, v.keep_b1, v.got_a1, v.got_b1, v.more_a1, v.more_b1, v.da0, v.db0, v.ga0, v.gb0
    v.end()

    other1 = swap(v.keep1, ZLO)
    la0 = swap(v.a0, Y1)
    lb0 = swap(v.b0, Y3)
    s1 = along_x(v.r1, 1)
    s3 = along_x(v.r3, 3)
    rows = [slice(0, 112), slice(112, 256), slice(256, 368), slice(368, 512)]
    v.up0, v.up1 = sums(*([(v.own, (r, EVERY)), (v.other_c, (r, EVERY))] for r in rows[2:]))
    v.other1, v.la0, v.lb0 = other1, la0, lb0
    del v.a0, v.b0, v.r1, v.r3
    v.end()

    v.da1, v.db1 = add_third(v.keep1, v.other1)
    v.lab0 = below(v.la0, v.lb0)
    v.s1, v.s3 = s1, s3
    del v.keep1, v.other1, v.la0, v.lb0
    v.end()

    ga1 = swap(v.da1, Y3)
    gb1 = swap(v.db1, Y1)
    back0 = to_section(v.up0)
    ab0_c = swap(v.ab0, CORE)
    lab0_c = swap(v.lab0, CORE)
    v.own_rows, v.hidden = normalize_backward(
        v.index, v.ours, v.rows, layer_norm_gain, [v.r0, v.s1, v.s3, v.s2]
    )
    v.ga1, v.gb1, v.ab0_c, v.lab0_c, v.back0 = ga1, gb1, ab0_c, lab0_c, back0
    del v.up0, v.r0, v.s1, v.s3, v.s2
    v.end()

    v.a1, v.b1, v.ab1 = join(v.da1, v.db1, v.ga1, v.gb1)
    del v.da1, v.db1, v.ga1, v.gb1
    v.end()

    la1 = swap(v.a1, Y1)
    lb1 = swap(v.b1, Y3)
    ab1_c = swap(v.ab1, CORE)
    hidden_c = swap(v.hidden, CORE)
    back1 = to_section(v.up1)
    v.weight_grad = finish(0, [v.ab0, v.ab0_c], [v.lab0, v.lab0_c], None)
    v.ab1_c, v.hidden_c = ab1_c, hidden_c
    v.weight_grad = finish(1, [v.ab1, v.ab1_c], [], v.weight_grad)
    v.result = both_taps(v.index, v.own_rows, v.hidden_c)
    v.la1, v.lb1, v.back1 = la1, lb1, back1
    del v.a1, v.b1, v.ab0, v.ab0_c, v.ab1, v.ab1_c, v.lab0, v.lab0_c, v.own_rows, v.hidden, v.hidden_c, v.up1
    v.end()

    la1_c = swap(v.la1, CORE)
    lb1_c = swap(v.lb1, CORE)
    projected = sums(
        *(
            [(v.own, (r, EVERY)), (v.other_c, (r, EVERY)), (back, (EVERY, EVERY))]
            for r, back in zip(rows, (v.back0, v.back1))
        ),
        stack=True,
    )[0]
    v.la1_c, v.lb1_c = la1_c, lb1_c
    v.weight_grad = finish(1, [], [v.la1, v.lb1, v.la1_c, v.lb1_c], v.weight_grad)
    return (projected[None], v.weight_grad, v.result)


def solution(mesh):
    return jax.shard_map(
        body,
        mesh=mesh,
        in_specs=(
            P("section", ("dp", "tensor"), None),
            P("section", None),
            P("section", None),
            P("section", "tensor"),
            P("dp", "section", "tensor"),
        ),
        out_specs=(
            P("dp", "section", "tensor"),
            P("section", "tensor"),
            P("section", ("dp", "tensor"), None),
        ),
        check_vma=False,
    )
```

```python
import jax
import jax.numpy as jnp
from jax import lax
from jax.experimental import pallas as pl
from jax.experimental.pallas import tpu as pltpu
from jax.sharding import PartitionSpec as P

F32 = jnp.float32
BF16 = jnp.bfloat16
VMEM_LIMIT = 20 * 1024 * 1024

ROW_CHUNKS = ((0, 640), (640, 640))


def dp_pairs(fy=lambda y: y, fz=lambda z: z, fc=lambda c: c):
    return [(i, fy(i // 4) * 4 + fz(i // 2 % 2) * 2 + fc(i % 2)) for i in range(16)]


Y1 = dp_pairs(fy=lambda y: y ^ 1)
Y3 = dp_pairs(fy=lambda y: y ^ 3)
ZLO = dp_pairs(fz=lambda z: z ^ 1)
CORE = dp_pairs(fc=lambda c: c ^ 1)
AROUND, SLOT_OF, SLOTS = 1, 5, 9


def swap(value, pairs):
    return lax.ppermute(value, "dp", pairs)


def along_x(value, step):
    return lax.ppermute(value, "tensor", [(i, (i + step) % 4) for i in range(4)])


def to_section(value):
    return lax.ppermute(value, "section", [(0, 1), (1, 0)])


ANY = pl.BlockSpec(memory_space=pl.ANY)
VMEM = pl.BlockSpec(memory_space=pltpu.VMEM)
SMEM = pl.BlockSpec(memory_space=pltpu.SMEM)


class Copies:
    def __init__(self, sems):
        self.sems, self.all = sems, []

    def start(self, *pairs):
        copies = []
        for source, target in pairs:
            copies.append(pltpu.make_async_copy(source, target, self.sems.at[len(self.all)]))
            copies[-1].start()
            self.all.append(copies[-1])
        return copies


def wait(*groups):
    for group in groups:
        for copy in group:
            copy.wait()


def call(kernel, operands, in_specs, out_shapes, out_specs, scratch=(), aliases=None):
    return pl.pallas_call(
        kernel,
        in_specs=in_specs,
        out_specs=out_specs,
        out_shape=out_shapes,
        scratch_shapes=scratch,
        input_output_aliases=aliases or {},
        compiler_params=pltpu.CompilerParams(vmem_limit_bytes=VMEM_LIMIT),
        cost_estimate=pl.CostEstimate(flops=1, bytes_accessed=1, transcendentals=0),
    )(*operands)


def prepare(features, cotangent):
    _, rows, width = features.shape
    _, tokens, cols = cotangent.shape
    part = cols // 4

    def kernel(features, cotangent, ours_out, theirs_out, mine_out, index_out, sems):
        s, d, x = lax.axis_index("section"), lax.axis_index("dp"), lax.axis_index("tensor")
        y, c = d // 4, d % 2
        around = (y, y + 1 - 2 * (y % 2), (y + 2) % 4, 3 - y)
        copies = Copies(sems)
        copies.start((features.at[c], ours_out), (features.at[1 - c], theirs_out))
        for n, j in enumerate(around):
            at = pl.ds(pl.multiple_of(j * part, part), part)
            copies.start((cotangent.at[0, :, at], mine_out.at[:, n * part : (n + 1) * part]))
        index_out[0] = c
        for n, j in enumerate(around):
            index_out[AROUND + n] = j
        for t in range(4):
            index_out[SLOT_OF + t] = (s if t < 2 else 1 - s) * 2 + t % 2
        for n, t in enumerate((x, (x + 1) % 4, (x + 3) % 4, (x + 2) % 4)):
            index_out[SLOTS + n] = ((t // 2 + s) % 2) * 2 + t % 2
        wait(copies.all)

    return call(
        kernel,
        [features, cotangent],
        [ANY, ANY],
        [out(rows, width), out(rows, width), out(tokens, cols), out(13, dtype=jnp.int32)],
        [VMEM, VMEM, VMEM, SMEM],
        [pltpu.SemaphoreType.DMA((6,))],
    )


def sums(*wanted, stack=False):
    arrays = []
    for terms in wanted:
        for array, _ in terms:
            if not any(array is a for a in arrays):
                arrays.append(array)
    places = [[(next(k for k, a in enumerate(arrays) if a is array), at) for array, at in terms] for terms in wanted]
    shapes = [out(*jax.eval_shape(lambda a, at=terms[0][1]: a[at], terms[0][0]).shape) for terms in wanted]
    made = [out(sum(s.shape[0] for s in shapes), *shapes[0].shape[1:])] if stack else shapes
    ends = [sum(s.shape[0] for s in shapes[: n + 1]) for n in range(len(shapes))]

    def kernel(*refs):
        ins, outs = refs[: len(arrays)], refs[len(arrays) :]
        for n, terms in enumerate(places):
            total = None
            for k, at in terms:
                value = ins[k][at].astype(F32)
                total = value if total is None else total + value
            if stack:
                outs[0][ends[n] - shapes[n].shape[0] : ends[n]] = total.astype(BF16)
            else:
                outs[n][...] = total.astype(BF16)

    return call(kernel, arrays, [VMEM] * len(arrays), made, [VMEM] * len(made))


def out(*shape, dtype=BF16):
    return jax.ShapeDtypeStruct(shape, dtype)


def dot(a, b, contract=(1, 0)):
    return lax.dot_general(a, b, (((contract[0],), (contract[1],)), ((), ())), preferred_element_type=F32)


def moments(value):
    mean = jnp.mean(value, axis=-1, keepdims=True)
    centered = value - mean
    inverse = 1.0 / jnp.sqrt(jnp.mean(centered * centered, axis=-1, keepdims=True) + 1e-05)
    return centered * inverse, inverse


def normalize(index, ours, theirs, gain, bias):
    rows = ours.shape[0]

    def kernel(index, ours, theirs, gain, bias, *outs):
        gain, bias = gain[pl.ds(index[0], 1)], bias[pl.ds(index[0], 1)]
        for k, value in enumerate((ours, theirs)):
            standard, _ = moments(value[...].astype(F32))
            normed = (standard * gain + bias).astype(BF16)
            for (start, size), out_ref in zip(ROW_CHUNKS, outs):
                out_ref[k] = normed[:, start : start + size]

    shapes = [out(2, rows, size) for _, size in ROW_CHUNKS]
    return call(kernel, [index, ours, theirs, gain, bias], [SMEM] + [VMEM] * 4, shapes, [VMEM] * len(shapes))


def normalize_backward(index, ours, theirs, gain, parts):
    count = len(parts)

    def kernel(index, ours, theirs, gain, *refs):
        gain = gain[pl.ds(index[0], 1)]
        for k, value in enumerate((ours, theirs)):
            standard, inverse = moments(value[...].astype(F32))
            total = refs[0][k].astype(F32)
            for ref in refs[1:count]:
                total = total + ref[k].astype(F32)
            scaled = total * gain
            hidden = inverse * (
                scaled
                - jnp.mean(scaled, axis=-1, keepdims=True)
                - standard * jnp.mean(scaled * standard, axis=-1, keepdims=True)
            )
            refs[count + k][...] = hidden.astype(BF16)

    shapes = [out(*ours.shape)] * 2
    return call(kernel, [index, ours, theirs, gain, *parts], [SMEM] + [VMEM] * (3 + count), shapes, [VMEM] * 2)


def both_taps(index, ours, theirs):
    def kernel(index, ours, theirs, result, sems):
        copies = Copies(sems)
        copies.start((ours, result.at[index[0]]), (theirs, result.at[1 - index[0]]))
        wait(copies.all)

    shape = out(2, *ours.shape)
    return call(
        kernel, [index, ours, theirs], [SMEM, VMEM, VMEM], [shape], [ANY], [pltpu.SemaphoreType.DMA((2,))]
    )[0]


def weight_grad_blocks(index, normed, grads, wanted):
    rows = normed[0].shape[-1]
    half = rows // 2
    part = grads[0].shape[1] // 4
    shapes = [out(half, blocks * part) for _, _, blocks in wanted]

    def kernel(index, *refs):
        ins, gs, outs, turned = refs[:4], refs[4:8], refs[8:-1], refs[-1]
        for t in range(4):
            for k in range(2):
                at = pl.multiple_of((4 * k + index[SLOTS + t]) * 128, 128)
                turned[:, pl.ds(at, 128)] = ins[t][k].T
        for (h, first, blocks), out_ref in zip(wanted, outs):
            mine = turned[h * half : (h + 1) * half]
            total = None
            for p in range(4):
                term = dot(mine[:, 256 * p : 256 * (p + 1)], gs[p][:, first * part : (first + blocks) * part])
                total = term if total is None else total + term
            out_ref[...] = total.astype(BF16)

    return call(
        kernel,
        [index, *normed, *grads],
        [SMEM] + [VMEM] * 8,
        shapes,
        [VMEM] * len(shapes),
        [pltpu.VMEM((rows, 1024), BF16)],
    )


def take_tap(index, proj_weight):
    width, cols = proj_weight.shape[0] // 2, proj_weight.shape[1]
    step = width // 8

    def kernel(index, weight, result, sems):
        copies = Copies(sems)
        for n in range(8):
            rows = pl.ds(pl.multiple_of(index[0] * width + n * step, step), step)
            copies.start((weight.at[rows], result.at[n * step : (n + 1) * step]))
        wait(copies.all)

    return call(
        kernel,
        [index, proj_weight],
        [SMEM, ANY],
        [out(width, cols)],
        [VMEM],
        [pltpu.SemaphoreType.DMA((8,))],
    )[0]


def row_gradients(index, grads, weight):
    width, cols = weight.shape
    part = cols // 4
    tile = 256

    def kernel(index, *refs):
        gs, w, outs, held, acc = refs[:4], refs[4], refs[5:9], refs[9], refs[10]
        for j in range(4):
            at = pl.multiple_of(index[AROUND + j] * part, part)
            for n in range(4):
                held[256 * n : 256 * (n + 1), pl.ds(at, part)] = gs[n][:, j * part : (j + 1) * part]
        for i in range(width // tile):
            here = slice(i * tile, (i + 1) * tile)
            acc[:, here] = dot(held[...], w[here], (1, 1)).astype(BF16)
        for t in range(4):
            for k in range(2):
                at = pl.multiple_of((4 * k + index[SLOTS + t]) * 128, 128)
                outs[t][k] = acc[pl.ds(at, 128)]

    return call(
        kernel,
        [index, *grads, weight],
        [SMEM] + [VMEM] * 5,
        [out(2, 128, width)] * 4,
        [VMEM] * 4,
        [pltpu.VMEM((1024, cols), BF16), pltpu.VMEM((1024, width), BF16)],
    )


def project(index, chunks, weight):
    width, cols = weight.shape
    part = cols // 4
    flat = [piece for chunk in chunks for piece in chunk]
    count = len(flat)

    def kernel(index, *refs):
        ins, w, own, other, held = refs[:count], refs[count], refs[count + 1], refs[count + 2], refs[count + 3]
        for m, (first, size) in enumerate(ROW_CHUNKS):
            for t in range(4):
                for k in range(2):
                    at = pl.multiple_of((4 * k + index[SLOTS + t]) * 128, 128)
                    held[pl.ds(at, 128), first : first + size] = ins[4 * m + t][k]
        for i in range(4):
            here = slice(i * part, (i + 1) * part)
            other[:, here] = dot(held[512:], w[:, here]).astype(BF16)
            own[:, here] = dot(held[:512], w[:, here]).astype(BF16)

    return call(
        kernel,
        [index, *flat, weight],
        [SMEM] + [VMEM] * (count + 1),
        [out(512, cols)] * 2,
        [VMEM] * 2,
        [pltpu.VMEM((1024, width), BF16)],
    )


EVERY = slice(None)


def add_first(next_a, next_b, got_a, got_b):
    part = next_a.shape[1]
    left, right = (EVERY, slice(0, part)), (EVERY, slice(part, 2 * part))
    return sums([(next_a, (EVERY, EVERY)), (got_a, right)], [(next_b, (EVERY, EVERY)), (got_b, left)])


def add_second(keep_a, keep_b, got_a, got_b, more_a, more_b):
    part = keep_a.shape[1]
    whole, left, right = (EVERY, EVERY), (EVERY, slice(0, part)), (EVERY, slice(part, 2 * part))
    return sums(
        [(keep_a, whole), (got_a, left), (more_a, whole)],
        [(keep_b, whole), (got_b, right), (more_b, whole)],
        stack=True,
    )[0]


def add_third(keep, other):
    half = keep.shape[0] // 2
    top, bottom = (slice(0, half), EVERY), (slice(half, 2 * half), EVERY)
    return sums([(keep, top), (other, top)], [(keep, bottom), (other, bottom)])


def join(left_a, left_b, right_a, right_b):
    half, part = left_a.shape

    def kernel(left_a, left_b, right_a, right_b, out_a, out_b, both):
        for n, (left, right, single) in enumerate(((left_a, right_a, out_a), (left_b, right_b, out_b))):
            rows = slice(n * half, (n + 1) * half)
            for source, here in ((left, slice(0, part)), (right, slice(part, 2 * part))):
                value = source[...]
                single[:, here] = value
                both[rows, here] = value

    return call(
        kernel,
        [left_a, left_b, right_a, right_b],
        [VMEM] * 4,
        [out(half, 2 * part), out(half, 2 * part), out(2 * half, 2 * part)],
        [VMEM] * 3,
    )


def below(top, bottom):
    rows = top.shape[0]

    def kernel(top, bottom, both):
        both[:rows] = top[...]
        both[rows:] = bottom[...]

    return call(kernel, [top, bottom], [VMEM] * 2, [out(2 * rows, top.shape[1])], [VMEM])[0]


def place(index, pieces, start, width, cols, into):
    part = cols // 4
    half = next(size for first, size in ROW_CHUNKS if first == start) // 2
    arrays = []
    for piece in pieces:
        if not any(piece[0] is a for a in arrays):
            arrays.append(piece[0])
    which = [next(k for k, a in enumerate(arrays) if a is piece[0]) for piece in pieces]
    count = len(arrays)

    def kernel(index, *refs):
        sources, result, sems = refs[:count], refs[-2], refs[-1]
        copies = Copies(sems)
        for k, (_, row, other, h, js) in zip(which, pieces):
            tap = 1 - index[0] if other else index[0]
            rows = pl.ds(pl.multiple_of(tap * width + start + h * half, 64), half)
            for n, j in enumerate(js):
                at = pl.ds(pl.multiple_of(index[AROUND + j] * part, part), part)
                copies.start((sources[k].at[row : row + half, n * part : (n + 1) * part], result.at[rows, at]))
        wait(copies.all)

    operands = [index, *arrays] + ([] if into is None else [into])
    return call(
        kernel,
        operands,
        [SMEM] + [VMEM] * count + ([] if into is None else [ANY]),
        [out(2 * width, cols)],
        [ANY],
        [pltpu.SemaphoreType.DMA((2 * len(pieces),))],
        {} if into is None else {count + 1: 0},
    )[0]


class Phases:
    def end(self):
        self.__dict__ = lax.optimization_barrier(self.__dict__)


def body(features, layer_norm_gain, layer_norm_bias, proj_weight, cotangent):
    width = layer_norm_gain.shape[1]
    cols = proj_weight.shape[1]
    half = ROW_CHUNKS[0][1] // 2
    wanted = ((0, 1, 2), (1, 2, 2), (0, 3, 1), (1, 1, 1), (0, 0, 1), (1, 0, 1))
    v = Phases()

    def grads():
        return [v.mine, v.away, v.mine_c, v.away_c]

    def finish(t, early, late, into):
        pieces = []
        for arrays, places in ((early, ((0, 3), (0, 1))), (late, ((1, 2), (3, 2)))):
            for n, array in enumerate(arrays):
                if len(arrays) == 2:
                    pieces += [(array, h * half, n == 1, h, places[h]) for h in range(2)]
                else:
                    pieces.append((array, 0, n > 1, n % 2, places[n % 2]))
        return place(v.index, pieces, ROW_CHUNKS[t][0], width, cols, into)

    v.ours, v.theirs, v.mine, v.index = prepare(features, cotangent)
    v.end()

    away = to_section(v.mine)
    rows = swap(v.theirs, CORE)
    mine_c = swap(v.mine, CORE)
    v.rows = rows
    v.n0, v.n1 = normalize(v.index, v.ours, v.rows, layer_norm_gain, layer_norm_bias)
    v.mine_c = mine_c
    del v.theirs
    v.end()

    x01 = along_x(v.n0, -1)
    x03 = along_x(v.n0, -3)
    x02 = along_x(v.n0, -2)
    v.weight = take_tap(v.index, proj_weight)
    v.x01, v.x03, v.x02, v.away = x01, x03, x02, away
    v.end()

    away_c = swap(v.away, CORE)
    x12 = along_x(v.n1, -2)
    v.away_c = away_c
    v.end()

    near0 = [v.n0, v.x01, v.x03, v.x02]
    v.send_a0, v.send_b0, v.next_a0, v.next_b0, v.keep_a0, v.keep_b0 = weight_grad_blocks(
        v.index, near0, grads(), wanted
    )
    v.x12 = x12
    v.end()

    got_a0 = swap(v.send_a0, Y1)
    got_b0 = swap(v.send_b0, Y3)
    x11 = along_x(v.n1, -1)
    x13 = along_x(v.n1, -3)
    v.r0, v.r1, v.r3, v.r2 = row_gradients(v.index, grads(), v.weight)
    v.got_a0, v.got_b0, v.x11, v.x13 = got_a0, got_b0, x11, x13
    del v.send_a0, v.send_b0
    v.end()

    v.n_a0, v.n_b0 = add_first(v.next_a0, v.next_b0, v.got_a0, v.got_b0)
    del v.next_a0, v.next_b0
    v.end()

    more_a0 = swap(v.n_a0, Y3)
    more_b0 = swap(v.n_b0, Y1)
    near1 = [v.n1, v.x11, v.x13, v.x12]
    v.send_a1, v.send_b1, v.next_a1, v.next_b1, v.keep_a1, v.keep_b1 = weight_grad_blocks(
        v.index, near1, grads(), wanted
    )
    v.more_a0, v.more_b0 = more_a0, more_b0
    del v.n_a0, v.n_b0, v.mine, v.away, v.mine_c, v.away_c
    v.end()

    v.keep0 = add_second(
        v.keep_a0, v.keep_b0, v.got_a0, v.got_b0, v.more_a0, v.more_b0
    )
    del v.keep_a0, v.keep_b0, v.got_a0, v.got_b0, v.more_a0, v.more_b0
    v.end()

    got_a1 = swap(v.send_a1, Y1)
    got_b1 = swap(v.send_b1, Y3)
    other0 = swap(v.keep0, ZLO)
    s2 = along_x(v.r2, 2)
    v.own, v.other = project(v.index, [[v.n0, v.x01, v.x03, v.x02], [v.n1, v.x11, v.x13, v.x12]], v.weight)
    v.got_a1, v.got_b1, v.other0 = got_a1, got_b1, other0
    del v.r2, v.send_a1, v.send_b1, v.x01, v.x03, v.x02, v.x11, v.x13, v.x12, v.n0, v.n1
    v.end()

    v.n_a1, v.n_b1 = add_first(v.next_a1, v.next_b1, v.got_a1, v.got_b1)
    v.da0, v.db0 = add_third(v.keep0, v.other0)
    v.s2 = s2
    del v.next_a1, v.next_b1, v.keep0, v.other0
    v.end()

    more_a1 = swap(v.n_a1, Y3)
    more_b1 = swap(v.n_b1, Y1)
    ga0 = swap(v.da0, Y3)
    gb0 = swap(v.db0, Y1)
    other_c = swap(v.other, CORE)
    v.more_a1, v.more_b1, v.ga0, v.gb0, v.other_c = more_a1, more_b1, ga0, gb0, other_c
    del v.n_a1, v.n_b1, v.other
    v.end()

    v.keep1 = add_second(
        v.keep_a1, v.keep_b1, v.got_a1, v.got_b1, v.more_a1, v.more_b1
    )
    v.a0, v.b0, v.ab0 = join(v.da0, v.db0, v.ga0, v.gb0)
    del v.keep_a1, v.keep_b1, v.got_a1, v.got_b1, v.more_a1, v.more_b1, v.da0, v.db0, v.ga0, v.gb0
    v.end()

    other1 = swap(v.keep1, ZLO)
    la0 = swap(v.a0, Y1)
    lb0 = swap(v.b0, Y3)
    s1 = along_x(v.r1, 1)
    s3 = along_x(v.r3, 3)
    rows = [slice(0, 112), slice(112, 256), slice(256, 368), slice(368, 512)]
    v.up0, v.up1 = sums(*([(v.own, (r, EVERY)), (v.other_c, (r, EVERY))] for r in rows[2:]))
    v.other1, v.la0, v.lb0 = other1, la0, lb0
    del v.a0, v.b0, v.r1, v.r3
    v.end()

    v.da1, v.db1 = add_third(v.keep1, v.other1)
    v.lab0 = below(v.la0, v.lb0)
    v.s1, v.s3 = s1, s3
    del v.keep1, v.other1, v.la0, v.lb0
    v.end()

    ga1 = swap(v.da1, Y3)
    gb1 = swap(v.db1, Y1)
    back0 = to_section(v.up0)
    ab0_c = swap(v.ab0, CORE)
    lab0_c = swap(v.lab0, CORE)
    v.own_rows, v.hidden = normalize_backward(
        v.index, v.ours, v.rows, layer_norm_gain, [v.r0, v.s1, v.s3, v.s2]
    )
    v.ga1, v.gb1, v.ab0_c, v.lab0_c, v.back0 = ga1, gb1, ab0_c, lab0_c, back0
    del v.up0, v.r0, v.s1, v.s3, v.s2
    v.end()

    v.a1, v.b1, v.ab1 = join(v.da1, v.db1, v.ga1, v.gb1)
    del v.da1, v.db1, v.ga1, v.gb1
    v.end()

    la1 = swap(v.a1, Y1)
    lb1 = swap(v.b1, Y3)
    ab1_c = swap(v.ab1, CORE)
    hidden_c = swap(v.hidden, CORE)
    back1 = to_section(v.up1)
    v.weight_grad = finish(0, [v.ab0, v.ab0_c], [v.lab0, v.lab0_c], None)
    v.ab1_c, v.hidden_c = ab1_c, hidden_c
    v.weight_grad = finish(1, [v.ab1, v.ab1_c], [], v.weight_grad)
    v.result = both_taps(v.index, v.own_rows, v.hidden_c)
    v.la1, v.lb1 = la1, lb1
    del v.a1, v.b1, v.ab0, v.ab0_c, v.ab1, v.ab1_c, v.lab0, v.lab0_c, v.own_rows, v.hidden, v.hidden_c, v.up1
    v.end()

    la1_c = swap(v.la1, CORE)
    lb1_c = swap(v.lb1, CORE)
    projected = sums(
        *(
            [(v.own, (r, EVERY)), (v.other_c, (r, EVERY)), (back, (EVERY, EVERY))]
            for r, back in zip(rows, (v.back0, back1))
        ),
        stack=True,
    )[0]
    v.la1_c, v.lb1_c = la1_c, lb1_c
    v.weight_grad = finish(1, [], [v.la1, v.lb1, v.la1_c, v.lb1_c], v.weight_grad)
    return (projected[None], v.weight_grad, v.result)


def solution(mesh):
    return jax.shard_map(
        body,
        mesh=mesh,
        in_specs=(
            P("section", ("dp", "tensor"), None),
            P("section", None),
            P("section", None),
            P("section", "tensor"),
            P("dp", "section", "tensor"),
        ),
        out_specs=(
            P("dp", "section", "tensor"),
            P("section", "tensor"),
            P("section", ("dp", "tensor"), None),
        ),
        check_vma=False,
    )
```

```python
import jax
import jax.numpy as jnp
from jax import lax
from jax.experimental import pallas as pl
from jax.experimental.pallas import tpu as pltpu
from jax.sharding import PartitionSpec as P

F32 = jnp.float32
BF16 = jnp.bfloat16
VMEM_LIMIT = 20 * 1024 * 1024

ROW_CHUNKS = ((0, 640), (640, 640))


def dp_pairs(fy=lambda y: y, fz=lambda z: z, fc=lambda c: c):
    return [(i, fy(i // 4) * 4 + fz(i // 2 % 2) * 2 + fc(i % 2)) for i in range(16)]


Y1 = dp_pairs(fy=lambda y: y ^ 1)
Y3 = dp_pairs(fy=lambda y: y ^ 3)
ZLO = dp_pairs(fz=lambda z: z ^ 1)
CORE = dp_pairs(fc=lambda c: c ^ 1)
AROUND, SLOT_OF, SLOTS = 1, 5, 9


def swap(value, pairs):
    return lax.ppermute(value, "dp", pairs)


def along_x(value, step):
    return lax.ppermute(value, "tensor", [(i, (i + step) % 4) for i in range(4)])


def to_section(value):
    return lax.ppermute(value, "section", [(0, 1), (1, 0)])


ANY = pl.BlockSpec(memory_space=pl.ANY)
VMEM = pl.BlockSpec(memory_space=pltpu.VMEM)
SMEM = pl.BlockSpec(memory_space=pltpu.SMEM)


class Copies:
    def __init__(self, sems):
        self.sems, self.all = sems, []

    def start(self, *pairs):
        copies = []
        for source, target in pairs:
            copies.append(pltpu.make_async_copy(source, target, self.sems.at[len(self.all)]))
            copies[-1].start()
            self.all.append(copies[-1])
        return copies


def wait(*groups):
    for group in groups:
        for copy in group:
            copy.wait()


def call(kernel, operands, in_specs, out_shapes, out_specs, scratch=(), aliases=None):
    return pl.pallas_call(
        kernel,
        in_specs=in_specs,
        out_specs=out_specs,
        out_shape=out_shapes,
        scratch_shapes=scratch,
        input_output_aliases=aliases or {},
        compiler_params=pltpu.CompilerParams(vmem_limit_bytes=VMEM_LIMIT),
        cost_estimate=pl.CostEstimate(flops=1, bytes_accessed=1, transcendentals=0),
    )(*operands)


def prepare(features, cotangent):
    _, rows, width = features.shape
    _, tokens, cols = cotangent.shape
    part = cols // 4

    def kernel(features, cotangent, ours_out, theirs_out, mine_out, index_out, sems):
        s, d, x = lax.axis_index("section"), lax.axis_index("dp"), lax.axis_index("tensor")
        y, c = d // 4, d % 2
        around = (y, y + 1 - 2 * (y % 2), (y + 2) % 4, 3 - y)
        copies = Copies(sems)
        copies.start((features.at[c], ours_out), (features.at[1 - c], theirs_out))
        for n, j in enumerate(around):
            at = pl.ds(pl.multiple_of(j * part, part), part)
            copies.start((cotangent.at[0, :, at], mine_out.at[:, n * part : (n + 1) * part]))
        index_out[0] = c
        for n, j in enumerate(around):
            index_out[AROUND + n] = j
        for t in range(4):
            index_out[SLOT_OF + t] = (s if t < 2 else 1 - s) * 2 + t % 2
        for n, t in enumerate((x, (x + 1) % 4, (x + 3) % 4, (x + 2) % 4)):
            index_out[SLOTS + n] = ((t // 2 + s) % 2) * 2 + t % 2
        wait(copies.all)

    return call(
        kernel,
        [features, cotangent],
        [ANY, ANY],
        [out(rows, width), out(rows, width), out(tokens, cols), out(13, dtype=jnp.int32)],
        [VMEM, VMEM, VMEM, SMEM],
        [pltpu.SemaphoreType.DMA((6,))],
    )


def sums(*wanted, stack=False):
    arrays = []
    for terms in wanted:
        for array, _ in terms:
            if not any(array is a for a in arrays):
                arrays.append(array)
    places = [[(next(k for k, a in enumerate(arrays) if a is array), at) for array, at in terms] for terms in wanted]
    shapes = [out(*jax.eval_shape(lambda a, at=terms[0][1]: a[at], terms[0][0]).shape) for terms in wanted]
    made = [out(sum(s.shape[0] for s in shapes), *shapes[0].shape[1:])] if stack else shapes
    ends = [sum(s.shape[0] for s in shapes[: n + 1]) for n in range(len(shapes))]

    def kernel(*refs):
        ins, outs = refs[: len(arrays)], refs[len(arrays) :]
        for n, terms in enumerate(places):
            total = None
            for k, at in terms:
                value = ins[k][at].astype(F32)
                total = value if total is None else total + value
            if stack:
                outs[0][ends[n] - shapes[n].shape[0] : ends[n]] = total.astype(BF16)
            else:
                outs[n][...] = total.astype(BF16)

    return call(kernel, arrays, [VMEM] * len(arrays), made, [VMEM] * len(made))


def out(*shape, dtype=BF16):
    return jax.ShapeDtypeStruct(shape, dtype)


def dot(a, b, contract=(1, 0)):
    return lax.dot_general(a, b, (((contract[0],), (contract[1],)), ((), ())), preferred_element_type=F32)


def moments(value):
    mean = jnp.mean(value, axis=-1, keepdims=True)
    centered = value - mean
    inverse = 1.0 / jnp.sqrt(jnp.mean(centered * centered, axis=-1, keepdims=True) + 1e-05)
    return centered * inverse, inverse


def normalize(index, ours, theirs, gain, bias):
    rows = ours.shape[0]

    def kernel(index, ours, theirs, gain, bias, *outs):
        gain, bias = gain[pl.ds(index[0], 1)], bias[pl.ds(index[0], 1)]
        for k, value in enumerate((ours, theirs)):
            standard, _ = moments(value[...].astype(F32))
            normed = (standard * gain + bias).astype(BF16)
            for (start, size), out_ref in zip(ROW_CHUNKS, outs):
                out_ref[k] = normed[:, start : start + size]

    shapes = [out(2, rows, size) for _, size in ROW_CHUNKS]
    return call(kernel, [index, ours, theirs, gain, bias], [SMEM] + [VMEM] * 4, shapes, [VMEM] * len(shapes))


def normalize_backward(index, ours, theirs, gain, parts):
    count = len(parts)

    def kernel(index, ours, theirs, gain, *refs):
        gain = gain[pl.ds(index[0], 1)]
        for k, value in enumerate((ours, theirs)):
            standard, inverse = moments(value[...].astype(F32))
            total = refs[0][k].astype(F32)
            for ref in refs[1:count]:
                total = total + ref[k].astype(F32)
            scaled = total * gain
            hidden = inverse * (
                scaled
                - jnp.mean(scaled, axis=-1, keepdims=True)
                - standard * jnp.mean(scaled * standard, axis=-1, keepdims=True)
            )
            refs[count + k][...] = hidden.astype(BF16)

    shapes = [out(*ours.shape)] * 2
    return call(kernel, [index, ours, theirs, gain, *parts], [SMEM] + [VMEM] * (3 + count), shapes, [VMEM] * 2)


def both_taps(index, ours, theirs):
    def kernel(index, ours, theirs, result, sems):
        copies = Copies(sems)
        copies.start((ours, result.at[index[0]]), (theirs, result.at[1 - index[0]]))
        wait(copies.all)

    shape = out(2, *ours.shape)
    return call(
        kernel, [index, ours, theirs], [SMEM, VMEM, VMEM], [shape], [ANY], [pltpu.SemaphoreType.DMA((2,))]
    )[0]


def weight_grad_blocks(index, normed, grads, wanted):
    rows = normed[0].shape[-1]
    half = rows // 2
    part = grads[0].shape[1] // 4
    shapes = [out(half, blocks * part) for _, _, blocks in wanted]

    def kernel(index, *refs):
        ins, gs, outs, turned = refs[:4], refs[4:8], refs[8:-1], refs[-1]
        for t in range(4):
            for k in range(2):
                at = pl.multiple_of((4 * k + index[SLOTS + t]) * 128, 128)
                turned[:, pl.ds(at, 128)] = ins[t][k].T
        for (h, first, blocks), out_ref in zip(wanted, outs):
            mine = turned[h * half : (h + 1) * half]
            total = None
            for p in range(4):
                term = dot(mine[:, 256 * p : 256 * (p + 1)], gs[p][:, first * part : (first + blocks) * part])
                total = term if total is None else total + term
            out_ref[...] = total.astype(BF16)

    return call(
        kernel,
        [index, *normed, *grads],
        [SMEM] + [VMEM] * 8,
        shapes,
        [VMEM] * len(shapes),
        [pltpu.VMEM((rows, 1024), BF16)],
    )


def take_tap(index, proj_weight):
    width, cols = proj_weight.shape[0] // 2, proj_weight.shape[1]
    step = width // 8

    def kernel(index, weight, result, sems):
        copies = Copies(sems)
        for n in range(8):
            rows = pl.ds(pl.multiple_of(index[0] * width + n * step, step), step)
            copies.start((weight.at[rows], result.at[n * step : (n + 1) * step]))
        wait(copies.all)

    return call(
        kernel,
        [index, proj_weight],
        [SMEM, ANY],
        [out(width, cols)],
        [VMEM],
        [pltpu.SemaphoreType.DMA((8,))],
    )[0]


def row_gradients(index, grads, weight):
    width, cols = weight.shape
    part = cols // 4
    tile = 256

    def kernel(index, *refs):
        gs, w, outs, held, acc = refs[:4], refs[4], refs[5:9], refs[9], refs[10]
        for j in range(4):
            at = pl.multiple_of(index[AROUND + j] * part, part)
            for n in range(4):
                held[256 * n : 256 * (n + 1), pl.ds(at, part)] = gs[n][:, j * part : (j + 1) * part]
        for i in range(width // tile):
            here = slice(i * tile, (i + 1) * tile)
            acc[:, here] = dot(held[...], w[here], (1, 1)).astype(BF16)
        for t in range(4):
            for k in range(2):
                at = pl.multiple_of((4 * k + index[SLOTS + t]) * 128, 128)
                outs[t][k] = acc[pl.ds(at, 128)]

    return call(
        kernel,
        [index, *grads, weight],
        [SMEM] + [VMEM] * 5,
        [out(2, 128, width)] * 4,
        [VMEM] * 4,
        [pltpu.VMEM((1024, cols), BF16), pltpu.VMEM((1024, width), BF16)],
    )


def project(index, chunks, weight):
    width, cols = weight.shape
    part = cols // 4
    flat = [piece for chunk in chunks for piece in chunk]
    count = len(flat)

    def kernel(index, *refs):
        ins, w, own, other, held = refs[:count], refs[count], refs[count + 1], refs[count + 2], refs[count + 3]
        for m, (first, size) in enumerate(ROW_CHUNKS):
            for t in range(4):
                for k in range(2):
                    at = pl.multiple_of((4 * k + index[SLOTS + t]) * 128, 128)
                    held[pl.ds(at, 128), first : first + size] = ins[4 * m + t][k]
        for i in range(4):
            here = slice(i * part, (i + 1) * part)
            other[:, here] = dot(held[512:], w[:, here]).astype(BF16)
            own[:, here] = dot(held[:512], w[:, here]).astype(BF16)

    return call(
        kernel,
        [index, *flat, weight],
        [SMEM] + [VMEM] * (count + 1),
        [out(512, cols)] * 2,
        [VMEM] * 2,
        [pltpu.VMEM((1024, width), BF16)],
    )


EVERY = slice(None)


def add_first(next_a, next_b, got_a, got_b):
    part = next_a.shape[1]
    left, right = (EVERY, slice(0, part)), (EVERY, slice(part, 2 * part))
    return sums([(next_a, (EVERY, EVERY)), (got_a, right)], [(next_b, (EVERY, EVERY)), (got_b, left)])


def add_second(keep_a, keep_b, got_a, got_b, more_a, more_b):
    part = keep_a.shape[1]
    whole, left, right = (EVERY, EVERY), (EVERY, slice(0, part)), (EVERY, slice(part, 2 * part))
    return sums(
        [(keep_a, whole), (got_a, left), (more_a, whole)],
        [(keep_b, whole), (got_b, right), (more_b, whole)],
        stack=True,
    )[0]


def add_third(keep, other):
    half = keep.shape[0] // 2
    top, bottom = (slice(0, half), EVERY), (slice(half, 2 * half), EVERY)
    return sums([(keep, top), (other, top)], [(keep, bottom), (other, bottom)])


def join(left_a, left_b, right_a, right_b):
    half, part = left_a.shape

    def kernel(left_a, left_b, right_a, right_b, out_a, out_b, both):
        for n, (left, right, single) in enumerate(((left_a, right_a, out_a), (left_b, right_b, out_b))):
            rows = slice(n * half, (n + 1) * half)
            for source, here in ((left, slice(0, part)), (right, slice(part, 2 * part))):
                value = source[...]
                single[:, here] = value
                both[rows, here] = value

    return call(
        kernel,
        [left_a, left_b, right_a, right_b],
        [VMEM] * 4,
        [out(half, 2 * part), out(half, 2 * part), out(2 * half, 2 * part)],
        [VMEM] * 3,
    )


def below(top, bottom):
    rows = top.shape[0]

    def kernel(top, bottom, both):
        both[:rows] = top[...]
        both[rows:] = bottom[...]

    return call(kernel, [top, bottom], [VMEM] * 2, [out(2 * rows, top.shape[1])], [VMEM])[0]


def place(index, pieces, start, width, cols, into):
    part = cols // 4
    half = next(size for first, size in ROW_CHUNKS if first == start) // 2
    arrays = []
    for piece in pieces:
        if not any(piece[0] is a for a in arrays):
            arrays.append(piece[0])
    which = [next(k for k, a in enumerate(arrays) if a is piece[0]) for piece in pieces]
    count = len(arrays)

    def kernel(index, *refs):
        sources, result, sems = refs[:count], refs[-2], refs[-1]
        copies = Copies(sems)
        for k, (_, row, other, h, js) in zip(which, pieces):
            tap = 1 - index[0] if other else index[0]
            rows = pl.ds(pl.multiple_of(tap * width + start + h * half, 64), half)
            for n, j in enumerate(js):
                at = pl.ds(pl.multiple_of(index[AROUND + j] * part, part), part)
                copies.start((sources[k].at[row : row + half, n * part : (n + 1) * part], result.at[rows, at]))
        wait(copies.all)

    operands = [index, *arrays] + ([] if into is None else [into])
    return call(
        kernel,
        operands,
        [SMEM] + [VMEM] * count + ([] if into is None else [ANY]),
        [out(2 * width, cols)],
        [ANY],
        [pltpu.SemaphoreType.DMA((2 * len(pieces),))],
        {} if into is None else {count + 1: 0},
    )[0]


class Phases:
    def end(self):
        self.__dict__ = lax.optimization_barrier(self.__dict__)


def body(features, layer_norm_gain, layer_norm_bias, proj_weight, cotangent):
    width = layer_norm_gain.shape[1]
    cols = proj_weight.shape[1]
    half = ROW_CHUNKS[0][1] // 2
    wanted = ((0, 1, 2), (1, 2, 2), (0, 3, 1), (1, 1, 1), (0, 0, 1), (1, 0, 1))
    v = Phases()

    def grads():
        return [v.mine, v.away, v.mine_c, v.away_c]

    def finish(t, early, late, into):
        pieces = []
        for arrays, places in ((early, ((0, 3), (0, 1))), (late, ((1, 2), (3, 2)))):
            for n, array in enumerate(arrays):
                if len(arrays) == 2:
                    pieces += [(array, h * half, n == 1, h, places[h]) for h in range(2)]
                else:
                    pieces.append((array, 0, n > 1, n % 2, places[n % 2]))
        return place(v.index, pieces, ROW_CHUNKS[t][0], width, cols, into)

    v.ours, v.theirs, v.mine, v.index = prepare(features, cotangent)
    v.end()

    away = to_section(v.mine)
    rows = swap(v.theirs, CORE)
    mine_c = swap(v.mine, CORE)
    v.rows = rows
    v.n0, v.n1 = normalize(v.index, v.ours, v.rows, layer_norm_gain, layer_norm_bias)
    v.mine_c = mine_c
    del v.theirs
    v.end()

    x01 = along_x(v.n0, -1)
    x03 = along_x(v.n0, -3)
    x02 = along_x(v.n0, -2)
    v.weight = take_tap(v.index, proj_weight)
    v.x01, v.x03, v.x02, v.away = x01, x03, x02, away
    v.end()

    away_c = swap(v.away, CORE)
    x12 = along_x(v.n1, -2)
    v.away_c = away_c
    v.end()

    near0 = [v.n0, v.x01, v.x03, v.x02]
    v.send_a0, v.send_b0, v.next_a0, v.next_b0, v.keep_a0, v.keep_b0 = weight_grad_blocks(
        v.index, near0, grads(), wanted
    )
    v.x12 = x12
    v.end()

    got_a0 = swap(v.send_a0, Y1)
    got_b0 = swap(v.send_b0, Y3)
    x11 = along_x(v.n1, -1)
    x13 = along_x(v.n1, -3)
    v.r0, v.r1, v.r3, v.r2 = row_gradients(v.index, grads(), v.weight)
    v.got_a0, v.got_b0, v.x11, v.x13 = got_a0, got_b0, x11, x13
    del v.send_a0, v.send_b0
    v.end()

    v.n_a0, v.n_b0 = add_first(v.next_a0, v.next_b0, v.got_a0, v.got_b0)
    del v.next_a0, v.next_b0
    v.end()

    more_a0 = swap(v.n_a0, Y3)
    more_b0 = swap(v.n_b0, Y1)
    near1 = [v.n1, v.x11, v.x13, v.x12]
    v.send_a1, v.send_b1, v.next_a1, v.next_b1, v.keep_a1, v.keep_b1 = weight_grad_blocks(
        v.index, near1, grads(), wanted
    )
    v.more_a0, v.more_b0 = more_a0, more_b0
    del v.n_a0, v.n_b0, v.mine, v.away, v.mine_c, v.away_c
    v.end()

    v.keep0 = add_second(
        v.keep_a0, v.keep_b0, v.got_a0, v.got_b0, v.more_a0, v.more_b0
    )
    del v.keep_a0, v.keep_b0, v.got_a0, v.got_b0, v.more_a0, v.more_b0
    v.end()

    got_a1 = swap(v.send_a1, Y1)
    got_b1 = swap(v.send_b1, Y3)
    other0 = swap(v.keep0, ZLO)
    s2 = along_x(v.r2, 2)
    v.own, v.other = project(v.index, [[v.n0, v.x01, v.x03, v.x02], [v.n1, v.x11, v.x13, v.x12]], v.weight)
    v.got_a1, v.got_b1, v.other0 = got_a1, got_b1, other0
    del v.r2, v.send_a1, v.send_b1, v.x01, v.x03, v.x02, v.x11, v.x13, v.x12, v.n0, v.n1
    v.end()

    v.n_a1, v.n_b1 = add_first(v.next_a1, v.next_b1, v.got_a1, v.got_b1)
    v.da0, v.db0 = add_third(v.keep0, v.other0)
    v.s2 = s2
    del v.next_a1, v.next_b1, v.keep0, v.other0
    v.end()

    more_a1 = swap(v.n_a1, Y3)
    more_b1 = swap(v.n_b1, Y1)
    ga0 = swap(v.da0, Y3)
    gb0 = swap(v.db0, Y1)
    other_c = swap(v.other, CORE)
    v.more_a1, v.more_b1, v.ga0, v.gb0, v.other_c = more_a1, more_b1, ga0, gb0, other_c
    del v.n_a1, v.n_b1, v.other
    v.end()

    v.keep1 = add_second(
        v.keep_a1, v.keep_b1, v.got_a1, v.got_b1, v.more_a1, v.more_b1
    )
    v.a0, v.b0, v.ab0 = join(v.da0, v.db0, v.ga0, v.gb0)
    del v.keep_a1, v.keep_b1, v.got_a1, v.got_b1, v.more_a1, v.more_b1, v.da0, v.db0, v.ga0, v.gb0
    v.end()

    other1 = swap(v.keep1, ZLO)
    la0 = swap(v.a0, Y1)
    lb0 = swap(v.b0, Y3)
    s1 = along_x(v.r1, 1)
    s3 = along_x(v.r3, 3)
    rows = [slice(0, 112), slice(112, 256), slice(256, 368), slice(368, 512)]
    v.up0, v.up1 = sums(*([(v.own, (r, EVERY)), (v.other_c, (r, EVERY))] for r in rows[2:]))
    v.other1, v.la0, v.lb0 = other1, la0, lb0
    del v.a0, v.b0, v.r1, v.r3
    v.end()

    v.da1, v.db1 = add_third(v.keep1, v.other1)
    v.lab0 = below(v.la0, v.lb0)
    v.s1, v.s3 = s1, s3
    del v.keep1, v.other1, v.la0, v.lb0
    v.end()

    ga1 = swap(v.da1, Y3)
    gb1 = swap(v.db1, Y1)
    back0 = to_section(v.up0)
    ab0_c = swap(v.ab0, CORE)
    lab0_c = swap(v.lab0, CORE)
    v.own_rows, v.hidden = normalize_backward(
        v.index, v.ours, v.rows, layer_norm_gain, [v.r0, v.s1, v.s3, v.s2]
    )
    v.ga1, v.gb1, v.ab0_c, v.lab0_c, v.back0 = ga1, gb1, ab0_c, lab0_c, back0
    del v.up0, v.r0, v.s1, v.s3, v.s2
    v.end()

    v.a1, v.b1, v.ab1 = join(v.da1, v.db1, v.ga1, v.gb1)
    del v.da1, v.db1, v.ga1, v.gb1
    v.end()

    la1 = swap(v.a1, Y1)
    lb1 = swap(v.b1, Y3)
    ab1_c = swap(v.ab1, CORE)
    hidden_c = swap(v.hidden, CORE)
    back1 = to_section(v.up1)
    v.weight_grad = finish(0, [v.ab0, v.ab0_c], [v.lab0, v.lab0_c], None)
    v.ab1_c, v.hidden_c = ab1_c, hidden_c
    v.weight_grad = finish(1, [v.ab1, v.ab1_c], [], v.weight_grad)
    v.result = both_taps(v.index, v.own_rows, v.hidden_c)
    v.la1, v.lb1, v.back1 = la1, lb1, back1
    del v.a1, v.b1, v.ab0, v.ab0_c, v.ab1, v.ab1_c, v.lab0, v.lab0_c, v.own_rows, v.hidden, v.hidden_c, v.up1
    v.end()

    la1_c = swap(v.la1, CORE)
    lb1_c = swap(v.lb1, CORE)
    projected = sums(
        *(
            [(v.own, (r, EVERY)), (v.other_c, (r, EVERY)), (back, (EVERY, EVERY))]
            for r, back in zip(rows, (v.back0, v.back1))
        ),
        stack=True,
    )[0]
    v.la1_c, v.lb1_c = la1_c, lb1_c
    v.weight_grad = finish(1, [], [v.la1, v.lb1, v.la1_c, v.lb1_c], v.weight_grad)
    return (projected[None], v.weight_grad, v.result)


def solution(mesh):
    return jax.shard_map(
        body,
        mesh=mesh,
        in_specs=(
            P("section", ("dp", "tensor"), None),
            P("section", None),
            P("section", None),
            P("section", "tensor"),
            P("dp", "section", "tensor"),
        ),
        out_specs=(
            P("dp", "section", "tensor"),
            P("section", "tensor"),
            P("section", ("dp", "tensor"), None),
        ),
        check_vma=False,
    )
```
